32 devices in a mesh: groups: 2 (over x), ctx: 4 (over y, core), head: 4 (over z).
Axes of the slice: x: 2, y: 2, z: 4, core: 2. Of those that a mesh axis runs over, the one named last changes fastest.
Arguments:
- cache_latent: bfloat16 [32768, 576], P(('groups', 'ctx')), parts along dimension 0, may hold values from -16 to 16
- index_key: bfloat16 [32768, 128], P(('groups', 'ctx')), parts along dimension 0, may hold values from -6 to 6
- query_latent: bfloat16 [512, 128, 576], P('groups', 'head'), parts along dimension 0, may hold values from -16 to 16
- index_query: bfloat16 [512, 64, 128], P('groups', 'head'), parts along dimension 0, may hold values from -6 to 6
- index_weight: bfloat16 [512, 64], P('groups', 'head'), parts along dimension 0, may hold values from -1 to 1
- block_ids: int32 [512, 32], P('groups'), parts along dimension 0, may hold values from 0 to 255, as said below
- stretch_start: int32 [2], P('groups'), parts along dimension 0, may hold values from 0 to 4095
Outputs:
- index_scores: float32 [32768, 256], P(('groups', 'ctx', 'head')), parts along dimension 0
- attended: bfloat16 [512, 128, 512], P(('groups', 'ctx'), 'head'), parts along dimension 0
The draws below stay inside these ranges and needn't reach their ends.
There are 2 independent parts, one for each index of `groups`. The reference program is written for one: setup_inputs(seed, part) draws one part's arguments, and reference() takes and returns one part's arrays. A program takes and returns all parts, laid end to end along the dimension named above; each array names one. Nothing has to cross between parts.
Inputs may be any that keep to these rules, and one draw needn't show every extreme that they name: `block_ids`: each row names 32 different blocks. Of the segments of 64 blocks (blocks o * 64 to o * 64 + 63), in each row a quarter hold exactly 16 of its blocks, a half hold 8 and a quarter none.
All inputs are finite; a program needn't handle non-finite values.
Results may differ from the reference program's by a relative error of at most 0.005.
Values may be sent and summed in bfloat16 or wider, within the bound.
No kernel may reach another device: no remote copies, remote signals or barrier semaphores. Data moves between devices by JAX's collectives and lax.ppermute only.
A program may use at most 192 MiB of HBM per device.

```python
import math
import jax
import jax.numpy as jnp
from jax import lax

H = 128
LATENT_WIDTH = 512
DR = 64
IH = 64
ID = 128
QKD = 192
BS = 64
TOPB = 32
ROWS = 256
SHARDS = 4
SLOTS = 16
BLK_DEV = 64
NBLK = 256
CONTEXT = 16384


def draw_cache_latent(key, part):
    key = jax.random.fold_in(key, 21)
    noise_key = jax.random.fold_in(key, 0)
    values = jnp.clip(jax.random.normal(noise_key, (CONTEXT, LATENT_WIDTH + DR), jnp.float32), -4.0, 4.0)
    return values.astype(jnp.bfloat16)


def draw_query_latent(key, part):
    key = jax.random.fold_in(key, 22)
    noise_key = jax.random.fold_in(key, 0)
    values = 0.5 * jnp.clip(jax.random.normal(noise_key, (ROWS, H, LATENT_WIDTH + DR), jnp.float32), -4.0, 4.0)
    return values.astype(jnp.bfloat16)


def draw_block_ids(key, part):
    key = jax.random.fold_in(key, 23)
    heat_key, noise_key, local_key = jax.random.split(key, 3)
    share = TOPB // SHARDS
    heat = jax.random.randint(heat_key, (SHARDS,), 0, 4)
    noise = jax.random.randint(noise_key, (ROWS, SHARDS), 0, 8)
    ranking = (noise + 3 * heat[None, :]) * SHARDS + jnp.arange(SHARDS, dtype=jnp.int32)[None, :]
    order = jnp.argsort(-ranking, axis=1, stable=True)
    place = jnp.argsort(order, axis=1, stable=True)
    quarter = SHARDS // 4
    counts = jnp.where(place < quarter, 2 * share, jnp.where(place < 3 * quarter, share, 0))
    local_rank = jax.random.randint(local_key, (ROWS, SHARDS, BLK_DEV), 0, 1 << 20) * BLK_DEV
    local_rank = local_rank + jnp.arange(BLK_DEV, dtype=jnp.int32)[None, None, :]
    picks = jnp.argsort(local_rank, axis=2, stable=True)[:, :, :SLOTS]
    block_numbers = picks + jnp.arange(SHARDS, dtype=jnp.int32)[None, :, None] * BLK_DEV
    live = jnp.arange(SLOTS, dtype=jnp.int32)[None, None, :] < counts[:, :, None]
    flat_numbers = block_numbers.reshape(ROWS, SHARDS * SLOTS)
    flat_live = live.reshape(ROWS, SHARDS * SLOTS)
    sorting = jnp.where(flat_live, 0, 1) * (SHARDS * SLOTS) + jnp.arange(SHARDS * SLOTS, dtype=jnp.int32)[None, :]
    chosen = jnp.argsort(sorting, axis=1, stable=True)[:, :TOPB]
    return jnp.take_along_axis(flat_numbers, chosen, axis=1).astype(jnp.int32)


def block_levels(own_key, dims, cuts, low, largest):
    gain, own = 1.0, jax.random.fold_in(own_key, 6)
    for axis_at, shards_of in cuts:
        draws = jnp.exp(jax.random.uniform(jax.random.fold_in(own, axis_at), (shards_of,), jnp.float32, low / len(cuts), largest / len(cuts)))
        gain = gain * jnp.repeat(draws, dims[axis_at] // shards_of).reshape([-1 if axis == axis_at else 1 for axis in range(len(dims))])
    return gain


def centred(key, extent, scale, bound, pieces=(), kind=jnp.bfloat16):
    values = scale * jax.random.normal(key, extent, jnp.float32)
    if pieces:
        values = values * block_levels(key, extent, pieces, -0.22, 0.18)
    return jnp.clip(values, -bound, bound).astype(kind)


def setup_inputs(seed: int = 0, part: int = 0) -> dict:
    key_of = jax.random.split(jax.random.key(seed), 8)
    part_keys = jax.random.split(jax.random.fold_in(key_of[7], part), 8)
    return {
        "cache_latent": draw_cache_latent(jax.random.fold_in(jax.random.fold_in(key_of[7], part), 71), part),
        "index_key": centred(part_keys[1], (CONTEXT, ID), 1.0, 6.0, ((0, 4),)),
        "query_latent": draw_query_latent(jax.random.fold_in(jax.random.fold_in(key_of[7], part), 71), part),
        "index_query": centred(part_keys[3], (ROWS, IH, ID), 1.0, 6.0, ((1, 4),)),
        "index_weight": centred(part_keys[4], (ROWS, IH), 0.25, 1.0, ((1, 4),)),
        "block_ids": draw_block_ids(jax.random.fold_in(jax.random.fold_in(key_of[7], part), 71), part),
        "stretch_start": jax.random.randint(part_keys[6], (1,), 0, 4096).astype(jnp.int32),
    }


NEG = -1.0e30


def rotate_rope(query, stretch_start):
    half = DR // 2
    positions = (stretch_start[0] + jnp.arange(query.shape[0], dtype=jnp.int32)).astype(jnp.float32)
    freqs = 10000.0 ** (-jnp.arange(half, dtype=jnp.float32) / half)
    angle = positions[:, None] * freqs[None, :]
    cosine = jnp.cos(angle)[:, None, :]
    sine = jnp.sin(angle)[:, None, :]
    first = query[..., LATENT_WIDTH:LATENT_WIDTH + half].astype(jnp.float32)
    second = query[..., LATENT_WIDTH + half:].astype(jnp.float32)
    turned = jnp.concatenate([first * cosine - second * sine, second * cosine + first * sine], axis=-1)
    return jnp.concatenate([query[..., :LATENT_WIDTH], turned.astype(jnp.bfloat16)], axis=-1)


def index_block(key_rows, index_query, index_weight):
    products = jnp.einsum('td,rhd->thr', key_rows.astype(jnp.float32), index_query.astype(jnp.float32)) * (ID ** -0.5)
    return jnp.einsum('thr,rh->tr', jnp.maximum(products, 0.0), index_weight.astype(jnp.float32))


def reference(cache_latent, index_key, query_latent, index_query, index_weight, block_ids, stretch_start):
    piece = math.gcd(CONTEXT, 512)
    key_blocks = index_key.reshape(CONTEXT // piece, piece, ID)
    index_scores = lax.map(lambda key_rows: index_block(key_rows, index_query, index_weight), key_blocks)
    index_scores = index_scores.reshape(CONTEXT, ROWS)

    cache_blocks = cache_latent.reshape(NBLK, BS, LATENT_WIDTH + DR)
    rotated = rotate_rope(query_latent, stretch_start)
    softmax_scale = QKD ** -0.5

    def one_row(operands):
        single_row_query, row_ids = operands
        gathered_latent_rows = cache_blocks[row_ids]
        attention_scores = jnp.einsum('jw,zrw->jzr', single_row_query.astype(jnp.float32), gathered_latent_rows.astype(jnp.float32)) * softmax_scale
        block_peak = jnp.max(attention_scores, axis=2)
        shard_of = row_ids // BLK_DEV
        same_shard = shard_of[:, None] == shard_of[None, :]
        same_float = same_shard.astype(jnp.float32)
        shard_peak = jnp.max(jnp.where(same_shard[None], block_peak[:, None, :], NEG), axis=2)
        weights = jnp.exp(attention_scores - shard_peak[:, :, None])
        rounded_values = lax.optimization_barrier(weights.astype(jnp.bfloat16)).astype(jnp.float32)
        top_peak = jnp.max(block_peak, axis=1)
        factor = jnp.exp(shard_peak - top_peak[:, None])
        block_numerator_part = jnp.einsum('vlj,lju->vlu', rounded_values, gathered_latent_rows[..., :LATENT_WIDTH].astype(jnp.float32))
        block_total = jnp.sum(weights, axis=2)
        seg_numer = jnp.einsum('hcd,bc->hbd', block_numerator_part, same_float)
        seg_total = jnp.einsum('hc,bc->hb', block_total, same_float)
        seg_out = (seg_numer / jnp.maximum(seg_total, 1.0)[:, :, None]).astype(jnp.bfloat16)
        seg_out = lax.optimization_barrier(seg_out).astype(jnp.float32)
        earlier = jnp.sum(jnp.tril(same_float, -1), axis=1)
        first = jnp.where(earlier == 0.0, 1.0, 0.0).astype(jnp.float32)
        seg_weight = factor * seg_total * first[None, :]
        numerator = jnp.einsum('hb,hbd->hd', seg_weight, seg_out)
        denominator = jnp.sum(seg_weight, axis=1)
        return (numerator / denominator[:, None]).astype(jnp.bfloat16)

    attended = lax.map(one_row, (rotated, block_ids))
    return (index_scores, attended)
```

```python
import functools

import jax
import jax.numpy as jnp
from jax import lax
from jax.experimental import pallas as pl
from jax.experimental.pallas import tpu as pltpu
from jax.sharding import PartitionSpec as P

LATENT_WIDTH = 512
DR = 64
ID = 128
QKD = 192
BS = 64
NEG = -1e30
EXP_SCALE = QKD**-0.5 * 1.4426950408889634
UNROLL = 4
VMEM_LIMIT = 58 * 2**20


def rope_part(query, stretch_start):
    half = DR // 2
    positions = (stretch_start[0] + jnp.arange(query.shape[0], dtype=jnp.int32)).astype(jnp.float32)
    freqs = 10000.0 ** (-jnp.arange(half, dtype=jnp.float32) / half)
    angle = positions[:, None] * freqs[None, :]
    cosine = jnp.cos(angle)[:, None, :]
    sine = jnp.sin(angle)[:, None, :]
    first = query[..., LATENT_WIDTH : LATENT_WIDTH + half].astype(jnp.float32)
    second = query[..., LATENT_WIDTH + half :].astype(jnp.float32)
    turned = jnp.concatenate(
        [first * cosine - second * sine, second * cosine + first * sine], axis=-1
    )
    return turned.astype(jnp.bfloat16)


def index_kernel(key_ref, query_ref, weight_ref, out_ref):
    keys = key_ref[...]
    total = None
    for head in range(query_ref.shape[0]):
        product = lax.dot_general(
            keys, query_ref[head], (((1,), (1,)), ((), ())), preferred_element_type=jnp.float32
        )
        term = jnp.maximum(product, 0.0) * weight_ref[head : head + 1, :]
        total = term if total is None else total + term
    out_ref[...] = total


def index_partial(index_key, index_query, index_weight):
    tokens = index_key.shape[0]
    rows, heads, width = index_query.shape
    tile = 256
    query = jnp.transpose(index_query, (1, 0, 2))
    weight = jnp.transpose(index_weight).astype(jnp.float32) * ID ** (-0.5)
    return pl.pallas_call(
        index_kernel,
        grid=(tokens // tile,),
        out_shape=jax.ShapeDtypeStruct((tokens, rows), jnp.float32),
        in_specs=[
            pl.BlockSpec((tile, width), lambda i: (i, 0)),
            pl.BlockSpec((heads, rows, width), lambda i: (0, 0, 0)),
            pl.BlockSpec((heads, rows), lambda i: (0, 0)),
        ],
        out_specs=pl.BlockSpec((tile, rows), lambda i: (i, 0)),
        compiler_params=pltpu.CompilerParams(vmem_limit_bytes=VMEM_LIMIT),
        cost_estimate=pl.CostEstimate(
            flops=4 * tokens * rows * heads * width,
            bytes_accessed=4 * tokens * rows,
            transcendentals=0,
        ),
        name="indexer",
    )(index_key, query, weight)


def attend_kernel(
    chunk,
    groups,
    offset_ref,
    count_ref,
    slot_ref,
    query_hbm,
    rope_hbm,
    own_hbm,
    peer_hbm,
    out_ref,
    top_ref,
    total_ref,
    cache_ref,
    turned_ref,
    query_ref,
    rope_ref,
    part_ref,
    stat_ref,
    item_ref,
    start_ref,
    sems,
):
    rows = query_ref.shape[0]
    heads = query_ref.shape[1]
    blocks = own_hbm.shape[0]
    offset = offset_ref[0]
    copies = [
        pltpu.make_async_copy(own_hbm, cache_ref.at[pl.ds(0, blocks)], sems.at[0]),
        pltpu.make_async_copy(peer_hbm, cache_ref.at[pl.ds(blocks, blocks)], sems.at[1]),
        pltpu.make_async_copy(query_hbm.at[pl.ds(offset, rows)], query_ref, sems.at[2]),
        pltpu.make_async_copy(rope_hbm.at[pl.ds(offset, rows)], rope_ref, sems.at[3]),
    ]
    for copy in copies:
        copy.start()

    def list_row(row, filled):
        start_ref[row] = filled
        for part in range(groups):
            item_ref[filled + part] = row * groups + part
        return filled + count_ref[0, offset + row]

    items = lax.fori_loop(0, rows, list_row, 0)

    def turn(block, carry):
        tokens = cache_ref[block]
        turned_ref[block] = jnp.concatenate([tokens, tokens], axis=0).T
        return carry

    copies[0].wait()
    lax.fori_loop(0, blocks, turn, 0)
    copies[1].wait()
    lax.fori_loop(blocks, 2 * blocks, turn, 0)
    copies[2].wait()
    copies[3].wait()

    lane = lax.broadcasted_iota(jnp.int32, (LATENT_WIDTH + DR, 2 * BS), 1)
    low_half = lane < BS

    def step(index, carry):
        done = []
        for unrolled in range(UNROLL):
            item = jnp.minimum(index * UNROLL + unrolled, items - 1)
            code = item_ref[item]
            row = code // groups
            part = code % groups
            names = [slot_ref[part * chunk + j, offset + row] for j in range(chunk)]
            keys = jnp.concatenate(
                [
                    jnp.where(low_half, turned_ref[names[j]], turned_ref[names[j + 1]])
                    for j in range(0, chunk, 2)
                ],
                axis=1,
            )
            values = jnp.concatenate(
                [cache_ref[name, :, :LATENT_WIDTH] for name in names], axis=0
            )
            scores = jnp.dot(
                query_ref[row, :, :LATENT_WIDTH],
                keys[:LATENT_WIDTH],
                preferred_element_type=jnp.float32,
            ) + jnp.dot(rope_ref[row], keys[LATENT_WIDTH:], preferred_element_type=jnp.float32)
            top = jnp.max(scores, axis=1, keepdims=True)
            weights = jnp.exp2((scores - top) * EXP_SCALE)
            total = jnp.sum(weights, axis=1, keepdims=True)
            numer = jnp.dot(
                weights.astype(jnp.bfloat16), values, preferred_element_type=jnp.float32
            )
            done.append((item, numer, top, total))
        for item, numer, top, total in done:
            part_ref[item] = numer
            stat_ref[0, item] = jnp.broadcast_to(top, (heads, 128))
            stat_ref[1, item] = jnp.broadcast_to(total, (heads, 128))
        return carry

    lax.fori_loop(0, (items + UNROLL - 1) // UNROLL, step, 0)

    out_lane = lax.broadcasted_iota(jnp.int32, (heads, 128), 1)
    wide = LATENT_WIDTH // 128

    def merge_row(row, carry):
        tops, totals = carry
        count = count_ref[0, offset + row]
        first = start_ref[row]
        places = [
            jnp.maximum(first + jnp.minimum(part, count - 1), 0) for part in range(groups)
        ]
        peaks = [
            jnp.where(part < count, stat_ref[0, places[part]], NEG) for part in range(groups)
        ]
        peak = functools.reduce(jnp.maximum, peaks)
        factors = [
            jnp.where(part < count, jnp.exp2((peaks[part] - peak) * EXP_SCALE), 0.0)
            for part in range(groups)
        ]
        total = sum(
            jnp.where(part < count, factors[part] * stat_ref[1, places[part]], 0.0)
            for part in range(groups)
        )
        inverse = jnp.where(count > 0, 1.0 / total, 0.0)
        merged = sum(
            jnp.where(
                part < count,
                part_ref[places[part]] * jnp.concatenate([factors[part] * inverse] * wide, axis=1),
                0.0,
            )
            for part in range(groups)
        )
        out_ref[row] = merged.astype(jnp.bfloat16)
        here = out_lane == row
        return jnp.where(here, peak, tops), jnp.where(here, total, totals)

    blank = jnp.zeros((heads, 128), jnp.float32)
    tops, totals = lax.fori_loop(0, rows, merge_row, (blank, blank))
    top_ref[...] = tops
    total_ref[...] = totals


def attend(offset, counts, slots, query, rope, own, peer, rows, chunk, groups):
    heads, width = query.shape[1], query.shape[2]
    blocks = own.shape[0]
    smem = pl.BlockSpec(memory_space=pltpu.SMEM)
    vmem = pl.BlockSpec(memory_space=pltpu.VMEM)
    hbm = pl.BlockSpec(memory_space=pl.ANY)
    items = rows * groups
    return pl.pallas_call(
        functools.partial(attend_kernel, chunk, groups),
        out_shape=(
            jax.ShapeDtypeStruct((rows, heads, LATENT_WIDTH), jnp.bfloat16),
            jax.ShapeDtypeStruct((heads, 128), jnp.float32),
            jax.ShapeDtypeStruct((heads, 128), jnp.float32),
        ),
        in_specs=[smem, smem, smem, hbm, hbm, hbm, hbm],
        out_specs=(vmem, vmem, vmem),
        scratch_shapes=[
            pltpu.VMEM((2 * blocks, BS, width), jnp.bfloat16),
            pltpu.VMEM((2 * blocks, width, 2 * BS), jnp.bfloat16),
            pltpu.VMEM((rows, heads, width), jnp.bfloat16),
            pltpu.VMEM((rows, heads, DR), jnp.bfloat16),
            pltpu.VMEM((items, heads, LATENT_WIDTH), jnp.float32),
            pltpu.VMEM((2, items, heads, 128), jnp.float32),
            pltpu.SMEM((items + groups,), jnp.int32),
            pltpu.SMEM((rows,), jnp.int32),
            pltpu.SemaphoreType.DMA((4,)),
        ],
        compiler_params=pltpu.CompilerParams(vmem_limit_bytes=VMEM_LIMIT),
        cost_estimate=pl.CostEstimate(
            flops=40 * 10**9, bytes_accessed=16 * 2**20, transcendentals=2 * 10**6
        ),
        name="attend",
    )(offset, counts, slots, query, rope, own, peer)


def chip_slots(block_ids, own_segment, peer_segment, blocks, chunk, groups):
    ids = jnp.transpose(block_ids)
    segment = ids // blocks
    local = ids % blocks
    place_of = jnp.where(segment == peer_segment, local + blocks, local)
    owned = (segment == own_segment) | (segment == peer_segment)
    count = ids.shape[0]
    before = jnp.tril(jnp.ones((count, count), jnp.float32), -1)
    place = jnp.dot(before, owned.astype(jnp.float32)).astype(jnp.int32)
    place = jnp.where(owned, place, -1)
    wanted = jnp.arange(groups * chunk, dtype=jnp.int32)
    slots = jnp.sum(
        jnp.where(place[:, None, :] == wanted[None, :, None], place_of[:, None, :], 0), axis=0
    )
    counts = jnp.sum(owned.astype(jnp.int32), axis=0, keepdims=True) // chunk
    return counts, slots


def per_device(
    cache_latent, index_key, query_latent, index_query, index_weight, block_ids, stretch_start
):
    shards = lax.axis_size("ctx")
    me = lax.axis_index("ctx")
    pairs = shards // 2
    core = me % 2
    pair = me // 2
    total_rows = query_latent.shape[0]
    rows = total_rows // shards
    chunk = block_ids.shape[1] // shards
    groups = 2 + min(2, shards // 4)
    blocks = cache_latent.shape[0] // BS

    own = cache_latent.reshape(blocks, BS, cache_latent.shape[1])
    peer = lax.ppermute(own, "ctx", [(i, i ^ 1) for i in range(shards)])
    partial = index_partial(index_key, index_query, index_weight)
    index_scores = lax.psum_scatter(partial, "head", scatter_dimension=0, tiled=True)

    rope = rope_part(query_latent, stretch_start)
    counts, slots = chip_slots(block_ids, me, me ^ 1, blocks, chunk, groups)

    def attend_for(owner):
        offset = (owner * rows).astype(jnp.int32).reshape(1)
        return attend(
            offset, counts, slots, query_latent, rope, own, peer, rows, chunk, groups
        )

    parts = []
    for ahead in range(1, pairs):
        owner = ((pair + ahead) % pairs) * 2 + core
        moves = [(i, ((i // 2 + ahead) % pairs) * 2 + i % 2) for i in range(shards)]
        parts.append([lax.ppermute(part, "ctx", moves) for part in attend_for(owner)])
    parts.append(attend_for(me))

    peak = functools.reduce(jnp.maximum, [part[1] for part in parts])
    shares = [jnp.exp2((part[1] - peak) * EXP_SCALE) * part[2] for part in parts]
    whole = sum(shares)
    attended = sum(
        part[0].astype(jnp.float32) * jnp.transpose((share / whole)[:, :rows])[:, :, None]
        for part, share in zip(parts, shares)
    )
    return (index_scores, attended.astype(jnp.bfloat16))


def solution(mesh):
    in_specs = (
        P(("groups", "ctx"), None),
        P(("groups", "ctx"), None),
        P("groups", "head", None),
        P("groups", "head", None),
        P("groups", "head"),
        P("groups", None),
        P("groups"),
    )
    out_specs = (P(("groups", "ctx", "head"), None), P(("groups", "ctx"), "head", None))
    return jax.shard_map(
        per_device, mesh=mesh, in_specs=in_specs, out_specs=out_specs, check_vma=False
    )
```

```python
import functools

import jax
import jax.numpy as jnp
from jax import lax
from jax.experimental import pallas as pl
from jax.experimental.pallas import tpu as pltpu
from jax.sharding import PartitionSpec as P

LATENT_WIDTH = 512
DR = 64
ID = 128
QKD = 192
BS = 64
NEG = -1e30
EXP_SCALE = QKD**-0.5 * 1.4426950408889634
UNROLL = 4
VMEM_LIMIT = 58 * 2**20


def rope_tables(rows, stretch_start):
    half = DR // 2
    positions = (stretch_start[0] + jnp.arange(rows, dtype=jnp.int32)).astype(jnp.float32)
    freqs = 10000.0 ** (-jnp.arange(half, dtype=jnp.float32) / half)
    angle = positions[None, :] * freqs[:, None]
    return jnp.cos(angle), jnp.sin(angle)


def index_kernel(key_ref, query_ref, weight_ref, out_ref):
    keys = key_ref[...]
    total = None
    for head in range(query_ref.shape[0]):
        product = lax.dot_general(
            keys, query_ref[head], (((1,), (1,)), ((), ())), preferred_element_type=jnp.float32
        )
        term = jnp.maximum(product, 0.0) * weight_ref[head : head + 1, :]
        total = term if total is None else total + term
    out_ref[...] = total


def index_partial(index_key, index_query, index_weight):
    tokens = index_key.shape[0]
    rows, heads, width = index_query.shape
    tile = 256
    query = jnp.transpose(index_query, (1, 0, 2))
    weight = jnp.transpose(index_weight).astype(jnp.float32) * ID ** (-0.5)
    return pl.pallas_call(
        index_kernel,
        grid=(tokens // tile,),
        out_shape=jax.ShapeDtypeStruct((tokens, rows), jnp.float32),
        in_specs=[
            pl.BlockSpec((tile, width), lambda i: (i, 0)),
            pl.BlockSpec((heads, rows, width), lambda i: (0, 0, 0)),
            pl.BlockSpec((heads, rows), lambda i: (0, 0)),
        ],
        out_specs=pl.BlockSpec((tile, rows), lambda i: (i, 0)),
        compiler_params=pltpu.CompilerParams(vmem_limit_bytes=VMEM_LIMIT),
        cost_estimate=pl.CostEstimate(
            flops=4 * tokens * rows * heads * width,
            bytes_accessed=4 * tokens * rows,
            transcendentals=0,
        ),
        name="indexer",
    )(index_key, query, weight)


def attend_kernel(
    chunk,
    groups,
    offset_ref,
    count_ref,
    slot_ref,
    query_hbm,
    cosine_ref,
    sine_ref,
    own_hbm,
    peer_hbm,
    out_ref,
    top_ref,
    total_ref,
    stage_ref,
    turned_ref,
    value_ref,
    raw_ref,
    query_ref,
    part_ref,
    stat_ref,
    item_ref,
    start_ref,
    sems,
):
    rows, heads, width = query_ref.shape
    tokens = own_hbm.shape[1]
    half = DR // 2
    piece = stage_ref.shape[2]
    pieces = 2 * tokens // piece
    offset = offset_ref[0]
    tile = pl.multiple_of(offset // 128 * 128, 128)
    inside = offset - tile

    def cache_copy(number):
        source = own_hbm if number * piece < tokens else peer_hbm
        return pltpu.make_async_copy(
            source.at[:, pl.ds(number * piece % tokens, piece)],
            stage_ref.at[number % 2],
            sems.at[number % 2],
        )

    query_copy = pltpu.make_async_copy(query_hbm.at[:, :, pl.ds(tile, 128)], raw_ref, sems.at[2])
    cache_copy(0).start()
    query_copy.start()
    cache_copy(1).start()

    def list_row(row, filled):
        start_ref[row] = filled
        for part in range(groups):
            item_ref[filled + part] = row * groups + part
        return filled + count_ref[0, offset + row]

    start_ref[rows] = lax.fori_loop(0, rows, list_row, 0)

    low_half = lax.broadcasted_iota(jnp.int32, (width, 2 * BS), 1) < BS

    for number in range(pieces):
        cache_copy(number).wait()

        def turn(index, carry, number=number):
            both = stage_ref[number % 2, :, pl.ds(pl.multiple_of(index * 128, 128), 128)]
            swapped = jnp.concatenate([both[:, BS:], both[:, :BS]], axis=1)
            block = number * (piece // BS) + 2 * index
            turned_ref[block] = jnp.where(low_half, both, swapped)
            turned_ref[block + 1] = jnp.where(low_half, swapped, both)
            values = both[:LATENT_WIDTH].T
            value_ref[block] = values[:BS]
            value_ref[block + 1] = values[BS:]
            return carry

        lax.fori_loop(0, piece // 128, turn, 0)
        if number + 2 < pieces:
            cache_copy(number + 2).start()

    query_copy.wait()
    cosine = cosine_ref[:, pl.ds(tile, 128)]
    sine = sine_ref[:, pl.ds(tile, 128)]

    def turn_query(block, carry):
        for head in range(8):
            raw = raw_ref[block * 8 + head].astype(jnp.float32)
            first = raw[LATENT_WIDTH : LATENT_WIDTH + half]
            second = raw[LATENT_WIDTH + half :]
            rotated = jnp.concatenate(
                [
                    raw[:LATENT_WIDTH],
                    first * cosine - second * sine,
                    second * cosine + first * sine,
                ],
                axis=0,
            ).T
            picked = rotated[:rows]
            for place in range(1, 128 // rows):
                picked = jnp.where(
                    inside == place * rows, rotated[place * rows : (place + 1) * rows], picked
                )
            query_ref[:, block * 8 + head, :] = picked
        return carry

    lax.fori_loop(0, heads // 8, turn_query, 0)

    out_lane = lax.broadcasted_iota(jnp.int32, (heads, 128), 1)
    wide = LATENT_WIDTH // 128
    batch = part_ref.shape[0] // groups

    def attend_batch(number, stats):
        base = start_ref[number * batch]
        stop = start_ref[(number + 1) * batch]

        def step(index, carry):
            done = []
            for unrolled in range(UNROLL):
                item = jnp.minimum(base + index * UNROLL + unrolled, stop - 1)
                code = item_ref[item]
                row = code // groups
                part = code % groups
                names = [slot_ref[part * chunk + j, offset + row] for j in range(chunk)]
                keys = jnp.concatenate(
                    [
                        jnp.where(low_half, turned_ref[names[j]], turned_ref[names[j + 1]])
                        for j in range(0, chunk, 2)
                    ],
                    axis=1,
                )
                values = jnp.concatenate([value_ref[name] for name in names], axis=0)
                scores = jnp.dot(
                    query_ref[row].astype(jnp.bfloat16), keys, preferred_element_type=jnp.float32
                )
                top = jnp.max(scores, axis=1, keepdims=True)
                weights = jnp.exp2((scores - top) * EXP_SCALE)
                total = jnp.sum(weights, axis=1, keepdims=True)
                numer = jnp.dot(
                    weights.astype(jnp.bfloat16), values, preferred_element_type=jnp.float32
                )
                done.append((item - base, numer, top, total))
            for item, numer, top, total in done:
                part_ref[item] = numer
                stat_ref[0, item] = jnp.broadcast_to(top, (heads, 128))
                stat_ref[1, item] = jnp.broadcast_to(total, (heads, 128))
            return carry

        lax.fori_loop(0, (stop - base + UNROLL - 1) // UNROLL, step, 0)

        def merge_row(index, carry):
            tops, totals = carry
            row = number * batch + index
            count = count_ref[0, offset + row]
            first = start_ref[row] - base
            places = [
                jnp.maximum(first + jnp.minimum(part, count - 1), 0) for part in range(groups)
            ]
            peaks = [
                jnp.where(part < count, stat_ref[0, places[part]], NEG) for part in range(groups)
            ]
            peak = functools.reduce(jnp.maximum, peaks)
            factors = [
                jnp.where(part < count, jnp.exp2((peaks[part] - peak) * EXP_SCALE), 0.0)
                for part in range(groups)
            ]
            total = sum(
                jnp.where(part < count, factors[part] * stat_ref[1, places[part]], 0.0)
                for part in range(groups)
            )
            inverse = jnp.where(count > 0, 1.0 / total, 0.0)
            merged = sum(
                jnp.where(
                    part < count,
                    part_ref[places[part]]
                    * jnp.concatenate([factors[part] * inverse] * wide, axis=1),
                    0.0,
                )
                for part in range(groups)
            )
            out_ref[row] = merged.astype(jnp.bfloat16)
            here = out_lane == row
            return jnp.where(here, peak, tops), jnp.where(here, total, totals)

        return lax.fori_loop(0, batch, merge_row, stats)

    blank = jnp.zeros((heads, 128), jnp.float32)
    tops, totals = lax.fori_loop(0, rows // batch, attend_batch, (blank, blank))
    top_ref[...] = tops
    total_ref[...] = totals


def attend(offset, counts, slots, query, cosine, sine, own, peer, rows, chunk, groups):
    heads, width = query.shape[0], query.shape[1]
    tokens = own.shape[1]
    blocks = tokens // BS
    smem = pl.BlockSpec(memory_space=pltpu.SMEM)
    vmem = pl.BlockSpec(memory_space=pltpu.VMEM)
    hbm = pl.BlockSpec(memory_space=pl.ANY)
    batch = min(rows, 32)
    return pl.pallas_call(
        functools.partial(attend_kernel, chunk, groups),
        out_shape=(
            jax.ShapeDtypeStruct((rows, heads, LATENT_WIDTH), jnp.bfloat16),
            jax.ShapeDtypeStruct((heads, 128), jnp.float32),
            jax.ShapeDtypeStruct((heads, 128), jnp.float32),
        ),
        in_specs=[smem, smem, smem, hbm, vmem, vmem, hbm, hbm],
        out_specs=(vmem, vmem, vmem),
        scratch_shapes=[
            pltpu.VMEM((2, width, tokens // 2), jnp.bfloat16),
            pltpu.VMEM((2 * blocks, width, 2 * BS), jnp.bfloat16),
            pltpu.VMEM((2 * blocks, BS, LATENT_WIDTH), jnp.bfloat16),
            pltpu.VMEM((heads, width, 128), jnp.bfloat16),
            pltpu.VMEM((rows, heads, width), jnp.float32),
            pltpu.VMEM((batch * groups, heads, LATENT_WIDTH), jnp.float32),
            pltpu.VMEM((2, batch * groups, heads, 128), jnp.float32),
            pltpu.SMEM((rows * groups + groups,), jnp.int32),
            pltpu.SMEM((rows + 1,), jnp.int32),
            pltpu.SemaphoreType.DMA((3,)),
        ],
        compiler_params=pltpu.CompilerParams(vmem_limit_bytes=VMEM_LIMIT),
        cost_estimate=pl.CostEstimate(
            flops=40 * 10**9, bytes_accessed=16 * 2**20, transcendentals=2 * 10**6
        ),
        name="attend",
    )(offset, counts, slots, query, cosine, sine, own, peer)


def chip_slots(block_ids, own_segment, peer_segment, blocks, chunk, groups):
    ids = jnp.transpose(block_ids)
    segment = ids // blocks
    local = ids % blocks
    place_of = jnp.where(segment == peer_segment, local + blocks, local)
    owned = (segment == own_segment) | (segment == peer_segment)
    count = ids.shape[0]
    before = jnp.tril(jnp.ones((count, count), jnp.float32), -1)
    place = jnp.dot(before, owned.astype(jnp.float32)).astype(jnp.int32)
    place = jnp.where(owned, place, -1)
    wanted = jnp.arange(groups * chunk, dtype=jnp.int32)
    slots = jnp.sum(
        jnp.where(place[:, None, :] == wanted[None, :, None], place_of[:, None, :], 0), axis=0
    )
    counts = jnp.sum(owned.astype(jnp.int32), axis=0, keepdims=True) // chunk
    return counts, slots


def per_device(
    cache_latent, index_key, query_latent, index_query, index_weight, block_ids, stretch_start
):
    shards = lax.axis_size("ctx")
    me = lax.axis_index("ctx")
    pairs = shards // 2
    core = me % 2
    pair = me // 2
    total_rows = query_latent.shape[0]
    rows = total_rows // shards
    chunk = block_ids.shape[1] // shards
    groups = 2 + min(2, shards // 4)
    blocks = cache_latent.shape[0] // BS

    own = jnp.transpose(cache_latent)
    peer = lax.ppermute(own, "ctx", [(i, i ^ 1) for i in range(shards)])
    partial = index_partial(index_key, index_query, index_weight)
    index_scores = lax.psum_scatter(partial, "head", scatter_dimension=0, tiled=True)

    query = jnp.transpose(query_latent, (1, 2, 0))
    cosine, sine = rope_tables(total_rows, stretch_start)
    counts, slots = chip_slots(block_ids, me, me ^ 1, blocks, chunk, groups)

    def attend_for(owner):
        offset = (owner * rows).astype(jnp.int32).reshape(1)
        return attend(
            offset, counts, slots, query, cosine, sine, own, peer, rows, chunk, groups
        )

    parts = []
    for ahead in range(1, pairs):
        owner = ((pair + ahead) % pairs) * 2 + core
        moves = [(i, ((i // 2 + ahead) % pairs) * 2 + i % 2) for i in range(shards)]
        parts.append([lax.ppermute(part, "ctx", moves) for part in attend_for(owner)])
    parts.append(attend_for(me))

    peak = functools.reduce(jnp.maximum, [part[1] for part in parts])
    shares = [jnp.exp2((part[1] - peak) * EXP_SCALE) * part[2] for part in parts]
    whole = sum(shares)
    attended = sum(
        part[0].astype(jnp.float32) * jnp.transpose((share / whole)[:, :rows])[:, :, None]
        for part, share in zip(parts, shares)
    )
    return (index_scores, attended.astype(jnp.bfloat16))


def solution(mesh):
    in_specs = (
        P(("groups", "ctx"), None),
        P(("groups", "ctx"), None),
        P("groups", "head", None),
        P("groups", "head", None),
        P("groups", "head"),
        P("groups", None),
        P("groups"),
    )
    out_specs = (P(("groups", "ctx", "head"), None), P(("groups", "ctx"), "head", None))
    return jax.shard_map(
        per_device, mesh=mesh, in_specs=in_specs, out_specs=out_specs, check_vma=False
    )
```

```python
import functools

import jax
import jax.numpy as jnp
from jax import lax
from jax.experimental import pallas as pl
from jax.experimental.pallas import tpu as pltpu
from jax.sharding import PartitionSpec as P

LATENT_WIDTH = 512
DR = 64
ID = 128
QKD = 192
BS = 64
NEG = -1e30
EXP_SCALE = QKD**-0.5 * 1.4426950408889634
UNROLL = 8
MERGE = 4
VMEM_LIMIT = 58 * 2**20


def rope_tables(rows, stretch_start):
    half = DR // 2
    positions = (stretch_start[0] + jnp.arange(rows, dtype=jnp.int32)).astype(jnp.float32)
    freqs = 10000.0 ** (-jnp.arange(half, dtype=jnp.float32) / half)
    angle = positions[None, :] * freqs[:, None]
    return jnp.cos(angle), jnp.sin(angle)


def index_kernel(place_ref, key_ref, query_ref, weight_ref, own_ref, sent_ref, wide_ref, turned_ref):
    del place_ref
    heads, _, rows = turned_ref.shape
    share = key_ref.shape[0]
    step = pl.program_id(0)

    @pl.when(step == 0)
    def _():
        wide_ref[...] = query_ref[...].astype(jnp.float32)
        for head in range(heads):
            turned_ref[head] = wide_ref[:, head, :].T.astype(jnp.bfloat16)

    weight = weight_ref[...].astype(jnp.float32) * ID ** (-0.5)

    def scores(first, count):
        keys = key_ref[pl.ds(first, count)]
        total = None
        for head in range(heads):
            product = jnp.dot(keys, turned_ref[head], preferred_element_type=jnp.float32)
            term = jnp.maximum(product, 0.0) * weight[head : head + 1, :]
            total = term if total is None else total + term
        return total

    count = min(share, 128)

    @pl.when(step == 0)
    def _():
        for first in range(0, share, count):
            own_ref[pl.ds(first, count)] = scores(first, count)

    @pl.when(step > 0)
    def _():
        for first in range(0, share, count):
            sent_ref[0, pl.ds(first, count)] = scores(first, count).astype(jnp.bfloat16)


def index_partial(index_key, index_query, index_weight, place, shards):
    tokens = index_key.shape[0]
    rows, heads, width = index_query.shape
    share = tokens // shards
    return pl.pallas_call(
        index_kernel,
        grid_spec=pltpu.PrefetchScalarGridSpec(
            num_scalar_prefetch=1,
            grid=(shards,),
            in_specs=[
                pl.BlockSpec((share, width), lambda i, at: (lax.rem(at[0] + i, shards), 0)),
                pl.BlockSpec((rows, heads, width), lambda i, at: (0, 0, 0)),
                pl.BlockSpec((heads, rows), lambda i, at: (0, 0)),
            ],
            out_specs=(
                pl.BlockSpec((share, rows), lambda i, at: (0, 0)),
                pl.BlockSpec((1, share, rows), lambda i, at: (jnp.maximum(i - 1, 0), 0, 0)),
            ),
            scratch_shapes=[
                pltpu.VMEM((rows, heads, width), jnp.float32),
                pltpu.VMEM((heads, width, rows), jnp.bfloat16),
            ],
        ),
        out_shape=(
            jax.ShapeDtypeStruct((share, rows), jnp.float32),
            jax.ShapeDtypeStruct((shards - 1, share, rows), jnp.bfloat16),
        ),
        compiler_params=pltpu.CompilerParams(vmem_limit_bytes=VMEM_LIMIT),
        cost_estimate=pl.CostEstimate(
            flops=4 * tokens * rows * heads * width,
            bytes_accessed=4 * tokens * rows,
            transcendentals=0,
        ),
        name="indexer",
    )(place, index_key, index_query, jnp.transpose(index_weight))


def attend_kernel(
    chunk,
    groups,
    offset_ref,
    count_ref,
    slot_ref,
    query_hbm,
    cosine_ref,
    sine_ref,
    own_hbm,
    peer_hbm,
    out_ref,
    top_ref,
    total_ref,
    stage_ref,
    turned_ref,
    value_ref,
    raw_ref,
    query_ref,
    part_ref,
    stat_ref,
    item_ref,
    start_ref,
    sems,
):
    rows, heads, width = query_ref.shape
    tokens = own_hbm.shape[1]
    half = DR // 2
    piece = stage_ref.shape[2]
    pieces = 2 * tokens // piece
    offset = offset_ref[0]
    tile = pl.multiple_of(offset // 128 * 128, 128)
    inside = offset - tile

    def cache_copy(number):
        source = own_hbm if number * piece < tokens else peer_hbm
        return pltpu.make_async_copy(
            source.at[:, pl.ds(number * piece % tokens, piece)],
            stage_ref.at[number % 2],
            sems.at[number % 2],
        )

    query_copy = pltpu.make_async_copy(query_hbm.at[:, :, pl.ds(tile, 128)], raw_ref, sems.at[2])
    cache_copy(0).start()
    query_copy.start()
    cache_copy(1).start()

    def list_row(row, filled):
        start_ref[row] = filled
        for part in range(groups):
            item_ref[filled + part] = row * groups + part
        return filled + count_ref[0, offset + row]

    start_ref[rows] = lax.fori_loop(0, rows, list_row, 0)

    deep = width
    low_half = lax.broadcasted_iota(jnp.int32, (deep, 2 * BS), 1) < BS

    for number in range(pieces):
        cache_copy(number).wait()

        def turn(index, carry, number=number):
            both = stage_ref[number % 2, :, pl.ds(pl.multiple_of(index * 128, 128), 128)]
            swapped = jnp.concatenate([both[:, BS:], both[:, :BS]], axis=1)
            block = number * (piece // BS) + 2 * index
            turned_ref[block] = jnp.where(low_half, both, swapped)
            turned_ref[block + 1] = jnp.where(low_half, swapped, both)
            values = both[:LATENT_WIDTH].T
            value_ref[block] = values[:BS]
            value_ref[block + 1] = values[BS:]
            return carry

        lax.fori_loop(0, piece // 128, turn, 0)
        if number + 2 < pieces:
            cache_copy(number + 2).start()

    query_copy.wait()
    cosine = cosine_ref[:, pl.ds(tile, 128)]
    sine = sine_ref[:, pl.ds(tile, 128)]

    def turn_query(block, carry):
        for head in range(8):
            raw = raw_ref[block * 8 + head].astype(jnp.float32)
            first = raw[LATENT_WIDTH : LATENT_WIDTH + half]
            second = raw[LATENT_WIDTH + half :]
            rotated = jnp.concatenate(
                [
                    raw[:LATENT_WIDTH],
                    first * cosine - second * sine,
                    second * cosine + first * sine,
                ],
                axis=0,
            ).T
            picked = rotated[:rows]
            for place in range(1, 128 // rows):
                picked = jnp.where(
                    inside == place * rows, rotated[place * rows : (place + 1) * rows], picked
                )
            query_ref[:, block * 8 + head, :] = picked
        return carry

    lax.fori_loop(0, heads // 8, turn_query, 0)

    out_lane = lax.broadcasted_iota(jnp.int32, (heads, 128), 1)
    wide = LATENT_WIDTH // 128
    batch = part_ref.shape[0] // groups

    def attend_batch(number, stats):
        base = start_ref[number * batch]
        stop = start_ref[(number + 1) * batch]

        def names_of(item):
            code = item_ref[item]
            row = code // groups
            part = code % groups
            return row, [slot_ref[part * chunk + j, offset + row] for j in range(chunk)]

        def scores_of(item):
            row, names = names_of(item)
            keys = jnp.concatenate(
                [
                    jnp.where(low_half, turned_ref[names[j]], turned_ref[names[j + 1]])
                    for j in range(0, chunk, 2)
                ],
                axis=1,
            )
            return jnp.dot(
                query_ref[row].astype(jnp.bfloat16), keys, preferred_element_type=jnp.float32
            )

        def softmax_of(scores):
            top = jnp.max(scores, axis=1, keepdims=True)
            weights = jnp.exp2((scores - top) * EXP_SCALE)
            return top, jnp.sum(weights, axis=1, keepdims=True), weights.astype(jnp.bfloat16)

        def numer_of(item, weights):
            _, names = names_of(item)
            values = jnp.concatenate([value_ref[name] for name in names], axis=0)
            return jnp.dot(weights, values, preferred_element_type=jnp.float32)

        def keep(item, top, total, numer):
            part_ref[item - base] = numer
            stat_ref[0, item - base] = jnp.broadcast_to(top, (heads, 128))
            stat_ref[1, item - base] = jnp.broadcast_to(total, (heads, 128))

        def item_at(index, unrolled):
            return jnp.minimum(base + index * UNROLL + unrolled, stop - 1)

        def step(index, carry):
            items = [item_at(index, u) for u in range(UNROLL)]
            scores = [scores_of(item) for item in items]
            soft = [softmax_of(s) for s in scores]
            numers = [numer_of(item, s[2]) for item, s in zip(items, soft)]
            for item, (top, total, _), numer in zip(items, soft, numers):
                keep(item, top, total, numer)
            return carry

        lax.fori_loop(0, (stop - base + UNROLL - 1) // UNROLL, step, 0)

        def merge_row(row):
            count = count_ref[0, offset + row]
            first = start_ref[row] - base
            places = [
                jnp.maximum(first + jnp.minimum(part, count - 1), 0) for part in range(groups)
            ]
            peaks = [
                jnp.where(part < count, stat_ref[0, places[part]], NEG) for part in range(groups)
            ]
            peak = functools.reduce(jnp.maximum, peaks)
            factors = [
                jnp.where(part < count, jnp.exp2((peaks[part] - peak) * EXP_SCALE), 0.0)
                for part in range(groups)
            ]
            total = sum(
                jnp.where(part < count, factors[part] * stat_ref[1, places[part]], 0.0)
                for part in range(groups)
            )
            inverse = jnp.where(count > 0, 1.0 / total, 0.0)
            merged = sum(
                jnp.where(
                    part < count,
                    part_ref[places[part]]
                    * jnp.concatenate([factors[part] * inverse] * wide, axis=1),
                    0.0,
                )
                for part in range(groups)
            )
            return merged.astype(jnp.bfloat16), peak, total

        def merge_rows(index, carry):
            tops, totals = carry
            found = [number * batch + index * MERGE + u for u in range(MERGE)]
            merged = [merge_row(row) for row in found]
            for row, (out, peak, total) in zip(found, merged):
                out_ref[row] = out
                here = out_lane == row
                tops = jnp.where(here, peak, tops)
                totals = jnp.where(here, total, totals)
            return tops, totals

        return lax.fori_loop(0, batch // MERGE, merge_rows, stats)

    blank = jnp.zeros((heads, 128), jnp.float32)
    tops, totals = lax.fori_loop(0, rows // batch, attend_batch, (blank, blank))
    top_ref[...] = tops
    total_ref[...] = totals


def attend(offset, counts, slots, query, cosine, sine, own, peer, rows, chunk, groups):
    heads, width = query.shape[0], query.shape[1]
    tokens = own.shape[1]
    blocks = tokens // BS
    smem = pl.BlockSpec(memory_space=pltpu.SMEM)
    vmem = pl.BlockSpec(memory_space=pltpu.VMEM)
    hbm = pl.BlockSpec(memory_space=pl.ANY)
    batch = min(rows, 32)
    return pl.pallas_call(
        functools.partial(attend_kernel, chunk, groups),
        out_shape=(
            jax.ShapeDtypeStruct((rows, heads, LATENT_WIDTH), jnp.bfloat16),
            jax.ShapeDtypeStruct((heads, 128), jnp.float32),
            jax.ShapeDtypeStruct((heads, 128), jnp.float32),
        ),
        in_specs=[smem, smem, smem, hbm, vmem, vmem, hbm, hbm],
        out_specs=(vmem, vmem, vmem),
        scratch_shapes=[
            pltpu.VMEM((2, width, tokens // 2), jnp.bfloat16),
            pltpu.VMEM((2 * blocks, width, 2 * BS), jnp.bfloat16),
            pltpu.VMEM((2 * blocks, BS, LATENT_WIDTH), jnp.bfloat16),
            pltpu.VMEM((heads, width, 128), jnp.bfloat16),
            pltpu.VMEM((rows, heads, width), jnp.float32),
            pltpu.VMEM((batch * groups, heads, LATENT_WIDTH), jnp.float32),
            pltpu.VMEM((2, batch * groups, heads, 128), jnp.float32),
            pltpu.SMEM((rows * groups + groups,), jnp.int32),
            pltpu.SMEM((rows + 1,), jnp.int32),
            pltpu.SemaphoreType.DMA((3,)),
        ],
        compiler_params=pltpu.CompilerParams(vmem_limit_bytes=VMEM_LIMIT),
        cost_estimate=pl.CostEstimate(
            flops=40 * 10**9, bytes_accessed=16 * 2**20, transcendentals=2 * 10**6
        ),
        name="attend",
    )(offset, counts, slots, query, cosine, sine, own, peer)


def chip_slots(block_ids, own_segment, peer_segment, blocks, chunk, groups):
    ids = jnp.transpose(block_ids)
    segment = ids // blocks
    local = ids % blocks
    place_of = jnp.where(segment == peer_segment, local + blocks, local)
    owned = (segment == own_segment) | (segment == peer_segment)
    count = ids.shape[0]
    before = jnp.tril(jnp.ones((count, count), jnp.float32), -1)
    place = jnp.dot(before, owned.astype(jnp.float32)).astype(jnp.int32)
    place = jnp.where(owned, place, -1)
    wanted = jnp.arange(groups * chunk, dtype=jnp.int32)
    slots = jnp.sum(
        jnp.where(place[:, None, :] == wanted[None, :, None], place_of[:, None, :], 0), axis=0
    )
    counts = jnp.sum(owned.astype(jnp.int32), axis=0, keepdims=True) // chunk
    return counts, slots


def per_device(
    cache_latent, index_key, query_latent, index_query, index_weight, block_ids, stretch_start
):
    shards = lax.axis_size("ctx")
    me = lax.axis_index("ctx")
    pairs = shards // 2
    core = me % 2
    pair = me // 2
    total_rows = query_latent.shape[0]
    rows = total_rows // shards
    chunk = block_ids.shape[1] // shards
    groups = 2 + min(2, shards // 4)
    blocks = cache_latent.shape[0] // BS

    own = jnp.transpose(cache_latent)
    peer = lax.ppermute(own, "ctx", [(i, i ^ 1) for i in range(shards)])
    head_shards = lax.axis_size("head")
    place = lax.axis_index("head").astype(jnp.int32).reshape(1)
    own_scores, sent = index_partial(index_key, index_query, index_weight, place, head_shards)
    come = [
        lax.ppermute(
            sent[ahead - 1], "head", [(i, (i + ahead) % head_shards) for i in range(head_shards)]
        )
        for ahead in range(1, head_shards)
    ]
    index_scores = own_scores + sum(part.astype(jnp.float32) for part in come)

    query = jnp.transpose(query_latent, (1, 2, 0))
    cosine, sine = rope_tables(total_rows, stretch_start)
    counts, slots = chip_slots(block_ids, me, me ^ 1, blocks, chunk, groups)

    def attend_for(owner):
        offset = (owner * rows).astype(jnp.int32).reshape(1)
        return attend(
            offset, counts, slots, query, cosine, sine, own, peer, rows, chunk, groups
        )

    parts = []
    for ahead in range(1, pairs):
        owner = ((pair + ahead) % pairs) * 2 + core
        moves = [(i, ((i // 2 + ahead) % pairs) * 2 + i % 2) for i in range(shards)]
        parts.append([lax.ppermute(part, "ctx", moves) for part in attend_for(owner)])
    parts.append(attend_for(me))

    peak = functools.reduce(jnp.maximum, [part[1] for part in parts])
    shares = [jnp.exp2((part[1] - peak) * EXP_SCALE) * part[2] for part in parts]
    whole = sum(shares)
    attended = sum(
        part[0].astype(jnp.float32) * jnp.transpose((share / whole)[:, :rows])[:, :, None]
        for part, share in zip(parts, shares)
    )
    return (index_scores, attended.astype(jnp.bfloat16))


def solution(mesh):
    in_specs = (
        P(("groups", "ctx"), None),
        P(("groups", "ctx"), None),
        P("groups", "head", None),
        P("groups", "head", None),
        P("groups", "head"),
        P("groups", None),
        P("groups"),
    )
    out_specs = (P(("groups", "ctx", "head"), None), P(("groups", "ctx"), "head", None))
    return jax.shard_map(
        per_device, mesh=mesh, in_specs=in_specs, out_specs=out_specs, check_vma=False
    )
```

```python
import functools

import jax
import jax.numpy as jnp
from jax import lax
from jax.experimental import pallas as pl
from jax.experimental.pallas import tpu as pltpu
from jax.sharding import PartitionSpec as P

LATENT_WIDTH = 512
DR = 64
ID = 128
QKD = 192
BS = 64
NEG = -1e30
EXP_SCALE = QKD**-0.5 * 1.4426950408889634
UNROLL = 8
MERGE = 4
VMEM_LIMIT = 58 * 2**20


def rope_tables(rows, stretch_start):
    half = DR // 2
    positions = (stretch_start[0] + jnp.arange(rows, dtype=jnp.int32)).astype(jnp.float32)
    freqs = 10000.0 ** (-jnp.arange(half, dtype=jnp.float32) / half)
    angle = positions[None, :] * freqs[:, None]
    return jnp.cos(angle), jnp.sin(angle)


def index_kernel(place_ref, key_ref, query_ref, weight_ref, own_ref, *rest):
    del place_ref
    sent_hbm, (wide_ref, turned_ref, sent_ref, sems) = rest[:-4], rest[-4:]
    heads, _, rows = turned_ref.shape
    share = key_ref.shape[0]
    step = pl.program_id(0)

    @pl.when(step == 0)
    def _():
        wide_ref[...] = query_ref[...].astype(jnp.float32)
        for head in range(heads):
            turned_ref[head] = wide_ref[:, head, :].T.astype(jnp.bfloat16)

    weight = weight_ref[...].astype(jnp.float32) * ID ** (-0.5)

    def scores(first, count):
        keys = key_ref[pl.ds(first, count)]
        total = None
        for head in range(heads):
            product = jnp.dot(keys, turned_ref[head], preferred_element_type=jnp.float32)
            term = jnp.maximum(product, 0.0) * weight[head : head + 1, :]
            total = term if total is None else total + term
        return total

    count = min(share, 128)

    @pl.when(step == 0)
    def _():
        for first in range(0, share, count):
            own_ref[pl.ds(first, count)] = scores(first, count)

    @pl.when(step > 0)
    def _():
        for first in range(0, share, count):
            sent_ref[step - 1, pl.ds(first, count)] = scores(first, count).astype(jnp.bfloat16)

    copies = [
        pltpu.make_async_copy(sent_ref.at[slot], target, sems.at[slot])
        for slot, target in enumerate(sent_hbm)
    ]
    for slot, copy in enumerate(copies):
        pl.when(step == slot + 1)(copy.start)

    @pl.when(step == len(copies))
    def _():
        for copy in copies:
            copy.wait()


def index_partial(index_key, index_query, index_weight, place, shards):
    tokens = index_key.shape[0]
    rows, heads, width = index_query.shape
    share = tokens // shards
    return pl.pallas_call(
        index_kernel,
        grid_spec=pltpu.PrefetchScalarGridSpec(
            num_scalar_prefetch=1,
            grid=(shards,),
            in_specs=[
                pl.BlockSpec((share, width), lambda i, at: (lax.rem(at[0] + i, shards), 0)),
                pl.BlockSpec((rows, heads, width), lambda i, at: (0, 0, 0)),
                pl.BlockSpec((heads, rows), lambda i, at: (0, 0)),
            ],
            out_specs=(
                pl.BlockSpec((share, rows), lambda i, at: (0, 0)),
            )
            + (pl.BlockSpec(memory_space=pl.ANY),) * (shards - 1),
            scratch_shapes=[
                pltpu.VMEM((rows, heads, width), jnp.float32),
                pltpu.VMEM((heads, width, rows), jnp.bfloat16),
                pltpu.VMEM((shards - 1, share, rows), jnp.bfloat16),
                pltpu.SemaphoreType.DMA((shards - 1,)),
            ],
        ),
        out_shape=(jax.ShapeDtypeStruct((share, rows), jnp.float32),)
        + (jax.ShapeDtypeStruct((share, rows), jnp.bfloat16),) * (shards - 1),
        compiler_params=pltpu.CompilerParams(vmem_limit_bytes=VMEM_LIMIT),
        cost_estimate=pl.CostEstimate(
            flops=4 * tokens * rows * heads * width,
            bytes_accessed=4 * tokens * rows,
            transcendentals=0,
        ),
        name="indexer",
    )(place, index_key, index_query, jnp.transpose(index_weight))


def attend_kernel(
    chunk,
    groups,
    offset_ref,
    count_ref,
    slot_ref,
    query_hbm,
    cosine_ref,
    sine_ref,
    own_hbm,
    peer_hbm,
    out_ref,
    level_ref,
    stage_ref,
    turned_ref,
    value_ref,
    raw_ref,
    query_ref,
    part_ref,
    stat_ref,
    item_ref,
    start_ref,
    sems,
):
    rows, heads, width = query_ref.shape
    tokens = own_hbm.shape[1]
    half = DR // 2
    piece = stage_ref.shape[2]
    pieces = 2 * tokens // piece
    offset = offset_ref[0]
    tile = pl.multiple_of(offset // 128 * 128, 128)
    inside = offset - tile

    def cache_copy(number):
        source = own_hbm if number * piece < tokens else peer_hbm
        return pltpu.make_async_copy(
            source.at[:, pl.ds(number * piece % tokens, piece)],
            stage_ref.at[number % 2],
            sems.at[number % 2],
        )

    query_copy = pltpu.make_async_copy(query_hbm.at[:, :, pl.ds(tile, 128)], raw_ref, sems.at[2])
    cache_copy(0).start()
    query_copy.start()
    cache_copy(1).start()

    def list_row(row, filled):
        start_ref[row] = filled
        for part in range(groups):
            item_ref[filled + part] = row * groups + part
        return filled + count_ref[0, offset + row]

    start_ref[rows] = lax.fori_loop(0, rows, list_row, 0)

    deep = width
    low_half = lax.broadcasted_iota(jnp.int32, (deep, 2 * BS), 1) < BS

    for number in range(pieces):
        cache_copy(number).wait()

        def turn(index, carry, number=number):
            both = stage_ref[number % 2, :, pl.ds(pl.multiple_of(index * 128, 128), 128)]
            swapped = jnp.concatenate([both[:, BS:], both[:, :BS]], axis=1)
            block = number * (piece // BS) + 2 * index
            turned_ref[block] = jnp.where(low_half, both, swapped)
            turned_ref[block + 1] = jnp.where(low_half, swapped, both)
            values = both[:LATENT_WIDTH].T
            value_ref[block] = values[:BS]
            value_ref[block + 1] = values[BS:]
            return carry

        lax.fori_loop(0, piece // 128, turn, 0)
        if number + 2 < pieces:
            cache_copy(number + 2).start()

    query_copy.wait()
    cosine = cosine_ref[:, pl.ds(tile, 128)]
    sine = sine_ref[:, pl.ds(tile, 128)]

    def turn_query(block, carry):
        for head in range(8):
            raw = raw_ref[block * 8 + head].astype(jnp.float32)
            first = raw[LATENT_WIDTH : LATENT_WIDTH + half]
            second = raw[LATENT_WIDTH + half :]
            rotated = jnp.concatenate(
                [
                    raw[:LATENT_WIDTH],
                    first * cosine - second * sine,
                    second * cosine + first * sine,
                ],
                axis=0,
            ).T
            picked = rotated[:rows]
            for place in range(1, 128 // rows):
                picked = jnp.where(
                    inside == place * rows, rotated[place * rows : (place + 1) * rows], picked
                )
            query_ref[:, block * 8 + head, :] = picked
        return carry

    lax.fori_loop(0, heads // 8, turn_query, 0)

    out_lane = lax.broadcasted_iota(jnp.int32, (heads, 128), 1)
    wide = LATENT_WIDTH // 128
    batch = part_ref.shape[0] // groups

    def attend_batch(number, stats):
        base = start_ref[number * batch]
        stop = start_ref[(number + 1) * batch]

        def names_of(item):
            code = item_ref[item]
            row = code // groups
            part = code % groups
            return row, [slot_ref[part * chunk + j, offset + row] for j in range(chunk)]

        def scores_of(item):
            row, names = names_of(item)
            keys = jnp.concatenate(
                [
                    jnp.where(low_half, turned_ref[names[j]], turned_ref[names[j + 1]])
                    for j in range(0, chunk, 2)
                ],
                axis=1,
            )
            return jnp.dot(
                query_ref[row].astype(jnp.bfloat16), keys, preferred_element_type=jnp.float32
            )

        def softmax_of(scores):
            top = jnp.max(scores, axis=1, keepdims=True)
            weights = jnp.exp2((scores - top) * EXP_SCALE)
            return top, jnp.sum(weights, axis=1, keepdims=True), weights.astype(jnp.bfloat16)

        def numer_of(item, weights):
            _, names = names_of(item)
            values = jnp.concatenate([value_ref[name] for name in names], axis=0)
            return jnp.dot(weights, values, preferred_element_type=jnp.float32)

        def keep(item, top, total, numer):
            part_ref[item - base] = numer
            stat_ref[0, item - base] = jnp.broadcast_to(top, (heads, 128))
            stat_ref[1, item - base] = jnp.broadcast_to(total, (heads, 128))

        def item_at(index, unrolled):
            return jnp.minimum(base + index * UNROLL + unrolled, stop - 1)

        def step(index, carry):
            items = [item_at(index, u) for u in range(UNROLL)]
            scores = [scores_of(item) for item in items]
            soft = [softmax_of(s) for s in scores]
            numers = [numer_of(item, s[2]) for item, s in zip(items, soft)]
            for item, (top, total, _), numer in zip(items, soft, numers):
                keep(item, top, total, numer)
            return carry

        lax.fori_loop(0, (stop - base + UNROLL - 1) // UNROLL, step, 0)

        def merge_row(row):
            count = count_ref[0, offset + row]
            first = start_ref[row] - base
            places = [
                jnp.maximum(first + jnp.minimum(part, count - 1), 0) for part in range(groups)
            ]
            peaks = [
                jnp.where(part < count, stat_ref[0, places[part]], NEG) for part in range(groups)
            ]
            peak = functools.reduce(jnp.maximum, peaks)
            factors = [
                jnp.where(part < count, jnp.exp2((peaks[part] - peak) * EXP_SCALE), 0.0)
                for part in range(groups)
            ]
            total = sum(
                jnp.where(part < count, factors[part] * stat_ref[1, places[part]], 0.0)
                for part in range(groups)
            )
            inverse = jnp.where(count > 0, 1.0 / total, 0.0)
            merged = sum(
                jnp.where(
                    part < count,
                    part_ref[places[part]]
                    * jnp.concatenate([factors[part] * inverse] * wide, axis=1),
                    0.0,
                )
                for part in range(groups)
            )
            return merged.astype(jnp.bfloat16), peak, total

        def merge_rows(index, carry):
            tops, totals = carry
            found = [number * batch + index * MERGE + u for u in range(MERGE)]
            merged = [merge_row(row) for row in found]
            for row, (out, peak, total) in zip(found, merged):
                out_ref[row] = out
                here = out_lane == row
                tops = jnp.where(here, peak, tops)
                totals = jnp.where(here, total, totals)
            return tops, totals

        return lax.fori_loop(0, batch // MERGE, merge_rows, stats)

    blank = jnp.zeros((heads, 128), jnp.float32)
    tops, totals = lax.fori_loop(0, rows // batch, attend_batch, (blank, blank))
    level_ref[0] = tops
    level_ref[1] = totals


def attend(offset, counts, slots, query, cosine, sine, own, peer, rows, chunk, groups):
    heads, width = query.shape[0], query.shape[1]
    tokens = own.shape[1]
    blocks = tokens // BS
    smem = pl.BlockSpec(memory_space=pltpu.SMEM)
    vmem = pl.BlockSpec(memory_space=pltpu.VMEM)
    hbm = pl.BlockSpec(memory_space=pl.ANY)
    batch = min(rows, 32)
    return pl.pallas_call(
        functools.partial(attend_kernel, chunk, groups),
        out_shape=(
            jax.ShapeDtypeStruct((rows, heads, LATENT_WIDTH), jnp.bfloat16),
            jax.ShapeDtypeStruct((2, heads, 128), jnp.float32),
        ),
        in_specs=[smem, smem, smem, hbm, vmem, vmem, hbm, hbm],
        out_specs=(vmem, vmem),
        scratch_shapes=[
            pltpu.VMEM((2, width, tokens // 2), jnp.bfloat16),
            pltpu.VMEM((2 * blocks, width, 2 * BS), jnp.bfloat16),
            pltpu.VMEM((2 * blocks, BS, LATENT_WIDTH), jnp.bfloat16),
            pltpu.VMEM((heads, width, 128), jnp.bfloat16),
            pltpu.VMEM((rows, heads, width), jnp.float32),
            pltpu.VMEM((batch * groups, heads, LATENT_WIDTH), jnp.float32),
            pltpu.VMEM((2, batch * groups, heads, 128), jnp.float32),
            pltpu.SMEM((rows * groups + groups,), jnp.int32),
            pltpu.SMEM((rows + 1,), jnp.int32),
            pltpu.SemaphoreType.DMA((3,)),
        ],
        compiler_params=pltpu.CompilerParams(vmem_limit_bytes=VMEM_LIMIT),
        cost_estimate=pl.CostEstimate(
            flops=40 * 10**9, bytes_accessed=16 * 2**20, transcendentals=2 * 10**6
        ),
        name="attend",
    )(offset, counts, slots, query, cosine, sine, own, peer)


def chip_slots(block_ids, own_segment, peer_segment, blocks, chunk, groups):
    ids = jnp.transpose(block_ids)
    segment = ids // blocks
    local = ids % blocks
    place_of = jnp.where(segment == peer_segment, local + blocks, local)
    owned = (segment == own_segment) | (segment == peer_segment)
    count = ids.shape[0]
    before = jnp.tril(jnp.ones((count, count), jnp.float32), -1)
    place = jnp.dot(before, owned.astype(jnp.float32)).astype(jnp.int32)
    place = jnp.where(owned, place, -1)
    wanted = jnp.arange(groups * chunk, dtype=jnp.int32)
    slots = jnp.sum(
        jnp.where(place[:, None, :] == wanted[None, :, None], place_of[:, None, :], 0), axis=0
    )
    counts = jnp.sum(owned.astype(jnp.int32), axis=0, keepdims=True) // chunk
    return counts, slots


def per_device(
    cache_latent, index_key, query_latent, index_query, index_weight, block_ids, stretch_start
):
    shards = lax.axis_size("ctx")
    me = lax.axis_index("ctx")
    pairs = shards // 2
    core = me % 2
    pair = me // 2
    total_rows = query_latent.shape[0]
    rows = total_rows // shards
    chunk = block_ids.shape[1] // shards
    groups = 2 + min(2, shards // 4)
    blocks = cache_latent.shape[0] // BS

    own = jnp.transpose(cache_latent)
    peer = lax.ppermute(own, "ctx", [(i, i ^ 1) for i in range(shards)])
    head_shards = lax.axis_size("head")
    place = lax.axis_index("head").astype(jnp.int32).reshape(1)
    own_scores, *sent = index_partial(index_key, index_query, index_weight, place, head_shards)
    come = [
        lax.ppermute(
            sent[ahead - 1], "head", [(i, (i + ahead) % head_shards) for i in range(head_shards)]
        )
        for ahead in range(1, head_shards)
    ]

    query = jnp.transpose(query_latent, (1, 2, 0))
    cosine, sine = rope_tables(total_rows, stretch_start)
    counts, slots = chip_slots(block_ids, me, me ^ 1, blocks, chunk, groups)

    def attend_for(owner):
        offset = (owner * rows).astype(jnp.int32).reshape(1)
        return attend(
            offset, counts, slots, query, cosine, sine, own, peer, rows, chunk, groups
        )

    parts = []
    for ahead in range(1, pairs):
        owner = ((pair + ahead) % pairs) * 2 + core
        moves = [(i, ((i // 2 + ahead) % pairs) * 2 + i % 2) for i in range(shards)]
        parts.append([lax.ppermute(part, "ctx", moves) for part in attend_for(owner)])
    parts.append(attend_for(me))

    come, parts[-1] = lax.optimization_barrier((come, parts[-1]))
    index_scores = own_scores + sum(part.astype(jnp.float32) for part in come)
    peak = functools.reduce(jnp.maximum, [part[1][0] for part in parts])
    shares = [jnp.exp2((part[1][0] - peak) * EXP_SCALE) * part[1][1] for part in parts]
    whole = sum(shares)
    attended = sum(
        part[0].astype(jnp.float32) * jnp.transpose((share / whole)[:, :rows])[:, :, None]
        for part, share in zip(parts, shares)
    )
    return (index_scores, attended.astype(jnp.bfloat16))


def solution(mesh):
    in_specs = (
        P(("groups", "ctx"), None),
        P(("groups", "ctx"), None),
        P("groups", "head", None),
        P("groups", "head", None),
        P("groups", "head"),
        P("groups", None),
        P("groups"),
    )
    out_specs = (P(("groups", "ctx", "head"), None), P(("groups", "ctx"), "head", None))
    return jax.shard_map(
        per_device, mesh=mesh, in_specs=in_specs, out_specs=out_specs, check_vma=False
    )
```

```python
import functools

import jax
import jax.numpy as jnp
from jax import lax
from jax.experimental import pallas as pl
from jax.experimental.pallas import tpu as pltpu
from jax.sharding import PartitionSpec as P

LATENT_WIDTH = 512
DR = 64
ID = 128
QKD = 192
BS = 64
NEG = -1e30
EXP_SCALE = QKD**-0.5 * 1.4426950408889634
UNROLL = 8
MERGE = 4
MOVE_COST = 44
VMEM_LIMIT = 58 * 2**20


def rope_tables(rows, stretch_start):
    half = DR // 2
    positions = (stretch_start[0] + jnp.arange(rows, dtype=jnp.int32)).astype(jnp.float32)
    freqs = 10000.0 ** (-jnp.arange(half, dtype=jnp.float32) / half)
    angle = positions[None, :] * freqs[:, None]
    return jnp.cos(angle), jnp.sin(angle)


def index_kernel(place_ref, key_ref, query_ref, weight_ref, own_ref, *rest):
    del place_ref
    sent_hbm, (wide_ref, turned_ref, sent_ref, sems) = rest[:-4], rest[-4:]
    heads, _, rows = turned_ref.shape
    share = key_ref.shape[0]
    step = pl.program_id(0)

    @pl.when(step == 0)
    def _():
        wide_ref[...] = query_ref[...].astype(jnp.float32)
        for head in range(heads):
            turned_ref[head] = wide_ref[:, head, :].T.astype(jnp.bfloat16)

    weight = weight_ref[...].astype(jnp.float32) * ID ** (-0.5)

    def scores(first, count):
        keys = key_ref[pl.ds(first, count)]
        total = None
        for head in range(heads):
            product = jnp.dot(keys, turned_ref[head], preferred_element_type=jnp.float32)
            term = jnp.maximum(product, 0.0) * weight[head : head + 1, :]
            total = term if total is None else total + term
        return total

    count = min(share, 128)

    @pl.when(step == 0)
    def _():
        for first in range(0, share, count):
            own_ref[pl.ds(first, count)] = scores(first, count)

    @pl.when(step > 0)
    def _():
        for first in range(0, share, count):
            sent_ref[step - 1, pl.ds(first, count)] = scores(first, count).astype(jnp.bfloat16)

    copies = [
        pltpu.make_async_copy(sent_ref.at[slot], target, sems.at[slot])
        for slot, target in enumerate(sent_hbm)
    ]
    for slot, copy in enumerate(copies):
        pl.when(step == slot + 1)(copy.start)

    @pl.when(step == len(copies))
    def _():
        for copy in copies:
            copy.wait()


def index_partial(index_key, index_query, index_weight, place, shards):
    tokens = index_key.shape[0]
    rows, heads, width = index_query.shape
    share = tokens // shards
    return pl.pallas_call(
        index_kernel,
        grid_spec=pltpu.PrefetchScalarGridSpec(
            num_scalar_prefetch=1,
            grid=(shards,),
            in_specs=[
                pl.BlockSpec((share, width), lambda i, at: (lax.rem(at[0] + i, shards), 0)),
                pl.BlockSpec((rows, heads, width), lambda i, at: (0, 0, 0)),
                pl.BlockSpec((heads, rows), lambda i, at: (0, 0)),
            ],
            out_specs=(
                pl.BlockSpec((share, rows), lambda i, at: (0, 0)),
            )
            + (pl.BlockSpec(memory_space=pl.ANY),) * (shards - 1),
            scratch_shapes=[
                pltpu.VMEM((rows, heads, width), jnp.float32),
                pltpu.VMEM((heads, width, rows), jnp.bfloat16),
                pltpu.VMEM((shards - 1, share, rows), jnp.bfloat16),
                pltpu.SemaphoreType.DMA((shards - 1,)),
            ],
        ),
        out_shape=(jax.ShapeDtypeStruct((share, rows), jnp.float32),)
        + (jax.ShapeDtypeStruct((share, rows), jnp.bfloat16),) * (shards - 1),
        compiler_params=pltpu.CompilerParams(vmem_limit_bytes=VMEM_LIMIT),
        cost_estimate=pl.CostEstimate(
            flops=4 * tokens * rows * heads * width,
            bytes_accessed=4 * tokens * rows,
            transcendentals=0,
        ),
        name="indexer",
    )(place, index_key, index_query, jnp.transpose(index_weight))


def attend_kernel(chunk, groups, sources, *refs):
    offset_ref, count_ref, slot_ref, query_hbm, cosine_ref, sine_ref = refs[:6]
    cache_hbm, refs = refs[6 : 6 + sources], refs[6 + sources :]
    out_ref, level_ref, stage_ref, turned_ref, value_ref, raw_ref, query_ref = refs[:7]
    part_ref, stat_ref, item_ref, start_ref, sems = refs[7:]
    rows, heads, width = query_ref.shape
    tokens = cache_hbm[0].shape[1]
    half = DR // 2
    piece = stage_ref.shape[2]
    pieces = sources * tokens // piece
    offset = offset_ref[0]
    tile = pl.multiple_of(offset // 128 * 128, 128)
    inside = offset - tile

    def cache_copy(number):
        source = cache_hbm[number * piece // tokens]
        return pltpu.make_async_copy(
            source.at[:, pl.ds(number * piece % tokens, piece)],
            stage_ref.at[number % 2],
            sems.at[number % 2],
        )

    query_copy = pltpu.make_async_copy(query_hbm.at[:, :, pl.ds(tile, 128)], raw_ref, sems.at[2])
    cache_copy(0).start()
    query_copy.start()
    cache_copy(1).start()

    def list_row(row, filled):
        start_ref[row] = filled
        for part in range(groups):
            item_ref[filled + part] = row * groups + part
        return filled + count_ref[0, offset + row]

    found = lax.fori_loop(0, rows, list_row, 0)
    start_ref[rows] = found

    deep = width
    low_half = lax.broadcasted_iota(jnp.int32, (deep, 2 * BS), 1) < BS

    for number in range(pieces):
        cache_copy(number).wait()

        def turn(index, carry, number=number):
            both = stage_ref[number % 2, :, pl.ds(pl.multiple_of(index * 128, 128), 128)]
            swapped = jnp.concatenate([both[:, BS:], both[:, :BS]], axis=1)
            block = number * (piece // BS) + 2 * index
            turned_ref[block] = jnp.where(low_half, both, swapped)
            turned_ref[block + 1] = jnp.where(low_half, swapped, both)
            values = both[:LATENT_WIDTH].T
            value_ref[block] = values[:BS]
            value_ref[block + 1] = values[BS:]
            return carry

        lax.fori_loop(0, jnp.where(found > 0, piece // 128, 0), turn, 0)
        if number + 2 < pieces:
            cache_copy(number + 2).start()

    query_copy.wait()
    cosine = cosine_ref[:, pl.ds(tile, 128)]
    sine = sine_ref[:, pl.ds(tile, 128)]

    def turn_query(block, carry):
        for head in range(8):
            raw = raw_ref[block * 8 + head].astype(jnp.float32)
            first = raw[LATENT_WIDTH : LATENT_WIDTH + half]
            second = raw[LATENT_WIDTH + half :]
            rotated = jnp.concatenate(
                [
                    raw[:LATENT_WIDTH],
                    first * cosine - second * sine,
                    second * cosine + first * sine,
                ],
                axis=0,
            ).T
            picked = rotated[:rows]
            for place in range(1, 128 // rows):
                picked = jnp.where(
                    inside == place * rows, rotated[place * rows : (place + 1) * rows], picked
                )
            query_ref[:, block * 8 + head, :] = picked
        return carry

    lax.fori_loop(0, jnp.where(found > 0, heads // 8, 0), turn_query, 0)

    out_lane = lax.broadcasted_iota(jnp.int32, (heads, 128), 1)
    wide = LATENT_WIDTH // 128
    batch = part_ref.shape[0] // groups

    def attend_batch(number, stats):
        base = start_ref[number * batch]
        stop = start_ref[(number + 1) * batch]

        def names_of(item):
            code = item_ref[item]
            row = code // groups
            part = code % groups
            return row, [slot_ref[part * chunk + j, offset + row] for j in range(chunk)]

        def scores_of(item):
            row, names = names_of(item)
            keys = jnp.concatenate(
                [
                    jnp.where(low_half, turned_ref[names[j]], turned_ref[names[j + 1]])
                    for j in range(0, chunk, 2)
                ],
                axis=1,
            )
            return jnp.dot(
                query_ref[row].astype(jnp.bfloat16), keys, preferred_element_type=jnp.float32
            )

        def softmax_of(scores):
            top = jnp.max(scores, axis=1, keepdims=True)
            weights = jnp.exp2((scores - top) * EXP_SCALE)
            return top, jnp.sum(weights, axis=1, keepdims=True), weights.astype(jnp.bfloat16)

        def numer_of(item, weights):
            _, names = names_of(item)
            values = jnp.concatenate([value_ref[name] for name in names], axis=0)
            return jnp.dot(weights, values, preferred_element_type=jnp.float32)

        def keep(item, top, total, numer):
            part_ref[item - base] = numer
            stat_ref[0, item - base] = jnp.broadcast_to(top, (heads, 128))
            stat_ref[1, item - base] = jnp.broadcast_to(total, (heads, 128))

        def item_at(index, unrolled):
            return jnp.minimum(base + index * UNROLL + unrolled, stop - 1)

        def step(index, carry):
            items = [item_at(index, u) for u in range(UNROLL)]
            scores = [scores_of(item) for item in items]
            soft = [softmax_of(s) for s in scores]
            numers = [numer_of(item, s[2]) for item, s in zip(items, soft)]
            for item, (top, total, _), numer in zip(items, soft, numers):
                keep(item, top, total, numer)
            return carry

        lax.fori_loop(0, (stop - base + UNROLL - 1) // UNROLL, step, 0)

        def merge_row(row):
            count = count_ref[0, offset + row]
            first = start_ref[row] - base
            places = [
                jnp.maximum(first + jnp.minimum(part, count - 1), 0) for part in range(groups)
            ]
            peaks = [
                jnp.where(part < count, stat_ref[0, places[part]], NEG) for part in range(groups)
            ]
            peak = functools.reduce(jnp.maximum, peaks)
            factors = [
                jnp.where(part < count, jnp.exp2((peaks[part] - peak) * EXP_SCALE), 0.0)
                for part in range(groups)
            ]
            total = sum(
                jnp.where(part < count, factors[part] * stat_ref[1, places[part]], 0.0)
                for part in range(groups)
            )
            inverse = jnp.where(count > 0, 1.0 / total, 0.0)
            merged = sum(
                jnp.where(
                    part < count,
                    part_ref[places[part]]
                    * jnp.concatenate([factors[part] * inverse] * wide, axis=1),
                    0.0,
                )
                for part in range(groups)
            )
            return merged.astype(jnp.bfloat16), peak, total

        def merge_rows(index, carry):
            tops, totals = carry
            found = [number * batch + index * MERGE + u for u in range(MERGE)]
            merged = [merge_row(row) for row in found]
            for row, (out, peak, total) in zip(found, merged):
                out_ref[row] = out
                here = out_lane == row
                tops = jnp.where(here, peak, tops)
                totals = jnp.where(here, total, totals)
            return tops, totals

        return lax.fori_loop(0, batch // MERGE, merge_rows, stats)

    blank = jnp.zeros((heads, 128), jnp.float32)
    tops, totals = lax.fori_loop(0, rows // batch, attend_batch, (blank, blank))
    level_ref[0] = tops
    level_ref[1] = totals


def attend(offset, counts, slots, query, cosine, sine, caches, rows, chunk, groups, work):
    heads, width = query.shape[0], query.shape[1]
    tokens = caches[0].shape[1]
    sources = len(caches)
    blocks = sources * tokens // BS
    piece = min(tokens, 2048)
    smem = pl.BlockSpec(memory_space=pltpu.SMEM)
    vmem = pl.BlockSpec(memory_space=pltpu.VMEM)
    hbm = pl.BlockSpec(memory_space=pl.ANY)
    batch = min(rows, 32)
    return pl.pallas_call(
        functools.partial(attend_kernel, chunk, groups, sources),
        out_shape=(
            jax.ShapeDtypeStruct((rows, heads, LATENT_WIDTH), jnp.bfloat16),
            jax.ShapeDtypeStruct((2, heads, 128), jnp.float32),
        ),
        in_specs=[smem, smem, smem, hbm, vmem, vmem] + [hbm] * sources,
        out_specs=(vmem, vmem),
        scratch_shapes=[
            pltpu.VMEM((2, width, piece), jnp.bfloat16),
            pltpu.VMEM((blocks, width, 2 * BS), jnp.bfloat16),
            pltpu.VMEM((blocks, BS, LATENT_WIDTH), jnp.bfloat16),
            pltpu.VMEM((heads, width, 128), jnp.bfloat16),
            pltpu.VMEM((rows, heads, width), jnp.float32),
            pltpu.VMEM((batch * groups, heads, LATENT_WIDTH), jnp.float32),
            pltpu.VMEM((2, batch * groups, heads, 128), jnp.float32),
            pltpu.SMEM((rows * groups + groups,), jnp.int32),
            pltpu.SMEM((rows + 1,), jnp.int32),
            pltpu.SemaphoreType.DMA((3,)),
        ],
        compiler_params=pltpu.CompilerParams(vmem_limit_bytes=VMEM_LIMIT),
        cost_estimate=pl.CostEstimate(
            flops=work, bytes_accessed=10**5, transcendentals=0
        ),
        name="attend",
    )(offset, counts, slots, query, cosine, sine, *caches)


def make_slots(owned, place_of, chunk, groups):
    count = owned.shape[0]
    before = jnp.tril(jnp.ones((count, count), jnp.float32), -1)
    place = jnp.dot(before, owned.astype(jnp.float32)).astype(jnp.int32)
    place = jnp.where(owned, place, -1)
    wanted = jnp.arange(groups * chunk, dtype=jnp.int32)
    slots = jnp.sum(
        jnp.where(place[:, None, :] == wanted[None, :, None], place_of[:, None, :], 0), axis=0
    )
    counts = jnp.sum(owned.astype(jnp.int32), axis=0, keepdims=True) // chunk
    return counts, slots


def plan_moves(segment, chunk, rows):
    numbers = jnp.arange(4, dtype=jnp.int32)
    hits = (segment[None] == numbers[:, None, None]).astype(jnp.int32)
    count = jnp.sum(hits, axis=1) // chunk
    owner = jnp.arange(segment.shape[1], dtype=jnp.int32) // rows
    core, pair = owner % 2, owner // 2
    lead = jnp.sum(count[2:], axis=0) - jnp.sum(count[:2], axis=0)
    leads = [jnp.sum(jnp.where(core == c, lead, 0)) for c in range(2)]
    heavy = (leads[0] + leads[1] > 0).astype(jnp.int32)
    sign = 2 * heavy - 1
    whole = jnp.sum(count, axis=1)
    hot = [2 * y + (whole[2 * y + 1] > whole[2 * y]).astype(jnp.int32) for y in range(2)]
    hot_heavy = jnp.where(heavy == 1, hot[1], hot[0])
    excess = jnp.where(core == 0, leads[0], leads[1]) * sign - MOVE_COST
    can = jnp.where(
        pair != heavy, jnp.sum(jnp.where(numbers[:, None] == hot_heavy, count, 0), axis=0), 0
    )
    index = jnp.arange(segment.shape[1], dtype=jnp.int32)
    earlier = (index[:, None] < index[None, :]) & (owner[:, None] == owner[None, :])
    before = jnp.sum(jnp.where(earlier, can[:, None], 0), axis=0)
    moved = (pair != heavy) & (2 * before < excess)
    return hot, hot_heavy, moved


def per_device(
    cache_latent, index_key, query_latent, index_query, index_weight, block_ids, stretch_start
):
    shards = lax.axis_size("ctx")
    me = lax.axis_index("ctx")
    pairs = shards // 2
    core = me % 2
    pair = me // 2
    total_rows = query_latent.shape[0]
    rows = total_rows // shards
    chunk = block_ids.shape[1] // shards
    groups = 2 + min(2, shards // 4)
    blocks = cache_latent.shape[0] // BS

    own = jnp.transpose(cache_latent)
    swap = [(i, i ^ 1) for i in range(shards)]
    peer = lax.ppermute(own, "ctx", swap)
    head_shards = lax.axis_size("head")
    place = lax.axis_index("head").astype(jnp.int32).reshape(1)
    own_scores, *sent = index_partial(index_key, index_query, index_weight, place, head_shards)
    come = [
        lax.ppermute(
            sent[ahead - 1], "head", [(i, (i + ahead) % head_shards) for i in range(head_shards)]
        )
        for ahead in range(1, head_shards)
    ]
    query = jnp.transpose(query_latent, (1, 2, 0))
    cosine, sine = rope_tables(total_rows, stretch_start)
    ids = jnp.transpose(block_ids)
    segment = ids // blocks
    local = ids % blocks
    place_of = jnp.where(segment == (me ^ 1), local + blocks, local)
    owned = segment // 2 == pair
    share_hot = pairs == 2
    if share_hot:
        hot, hot_heavy, moved = plan_moves(segment, chunk, rows)
        owned &= ~(moved[None, :] & (segment == hot_heavy))
        my_hot = jnp.where(pair == 1, hot[1], hot[0])
        quarter = own.shape[1] // 4
        near = []
        for number in range(2):
            at = (2 * core + number) * quarter
            sent_piece = jnp.where(
                my_hot == me,
                lax.dynamic_slice_in_dim(own, at, quarter, 1),
                lax.dynamic_slice_in_dim(peer, at, quarter, 1),
            )
            near.append(lax.ppermute(sent_piece, "ctx", [(i, i ^ 2) for i in range(shards)]))
        moved_place = jnp.where(
            local // (blocks // 2) == core, local % (blocks // 2), local % (blocks // 2) + blocks // 2
        )
        more_counts, more_slots = make_slots(
            moved[None, :] & (segment == hot_heavy), moved_place, chunk, groups
        )
    counts, slots = make_slots(owned, place_of, chunk, groups)

    if share_hot:
        counts, own_scores = lax.optimization_barrier((counts, own_scores))

    def attend_for(owner, work, counts, slots, *caches):
        offset = (owner * rows).astype(jnp.int32).reshape(1)
        return attend(
            offset, counts, slots, query, cosine, sine, caches, rows, chunk, groups, work
        )

    parts = []
    for ahead in range(1, pairs):
        owner = ((pair + ahead) % pairs) * 2 + core
        moves = [(i, ((i // 2 + ahead) % pairs) * 2 + i % 2) for i in range(shards)]
        result = attend_for(owner, 40 * 10**9, counts, slots, own, peer)
        counts, result, come = lax.optimization_barrier((counts, result, come))
        parts.append([lax.ppermute(part, "ctx", moves) for part in result])
    mine = attend_for(me, 10**7, counts, slots, own, peer)
    if share_hot:
        near, mine, parts[0][1] = lax.optimization_barrier((near, mine, parts[0][1]))
        far = [lax.ppermute(piece, "ctx", swap) for piece in near]
    parts.append(mine)

    if share_hot:
        more_counts, parts = lax.optimization_barrier((more_counts, parts))
        parts.append(attend_for(me, 10**7, more_counts, more_slots, *near, *far))

    come, parts[-1] = lax.optimization_barrier((come, parts[-1]))
    index_scores = own_scores + sum(part.astype(jnp.float32) for part in come)
    peak = functools.reduce(jnp.maximum, [part[1][0] for part in parts])
    shares = [jnp.exp2((part[1][0] - peak) * EXP_SCALE) * part[1][1] for part in parts]
    whole = sum(shares)
    attended = sum(
        part[0].astype(jnp.float32) * jnp.transpose((share / whole)[:, :rows])[:, :, None]
        for part, share in zip(parts, shares)
    )
    return (index_scores, attended.astype(jnp.bfloat16))


def solution(mesh):
    in_specs = (
        P(("groups", "ctx"), None),
        P(("groups", "ctx"), None),
        P("groups", "head", None),
        P("groups", "head", None),
        P("groups", "head"),
        P("groups", None),
        P("groups"),
    )
    out_specs = (P(("groups", "ctx", "head"), None), P(("groups", "ctx"), "head", None))
    return jax.shard_map(
        per_device, mesh=mesh, in_specs=in_specs, out_specs=out_specs, check_vma=False
    )
```

```python
import functools

import jax
import jax.numpy as jnp
from jax import lax
from jax.experimental import pallas as pl
from jax.experimental.pallas import tpu as pltpu
from jax.sharding import PartitionSpec as P

LATENT_WIDTH = 512
DR = 64
ID = 128
QKD = 192
BS = 64
NEG = -1e30
EXP_SCALE = QKD**-0.5 * 1.4426950408889634
UNROLL = 8
MERGE = 4
VMEM_LIMIT = 58 * 2**20


def rope_tables(rows, stretch_start):
    half = DR // 2
    positions = (stretch_start[0] + jnp.arange(rows, dtype=jnp.int32)).astype(jnp.float32)
    freqs = 10000.0 ** (-jnp.arange(half, dtype=jnp.float32) / half)
    angle = positions[None, :] * freqs[:, None]
    return jnp.cos(angle), jnp.sin(angle)


def index_kernel(key_ref, query_ref, weight_ref, out_ref, wide_ref, turned_ref):
    heads = turned_ref.shape[0]
    tile = key_ref.shape[0]

    @pl.when(pl.program_id(0) == 0)
    def _():
        wide_ref[...] = query_ref[...].astype(jnp.float32)
        for head in range(heads):
            turned_ref[head] = wide_ref[:, head, :].T.astype(jnp.bfloat16)

    weight = weight_ref[...].astype(jnp.float32) * ID ** (-0.5)
    count = min(tile, 128)
    for first in range(0, tile, count):
        keys = key_ref[pl.ds(first, count)]
        total = None
        for head in range(heads):
            product = jnp.dot(keys, turned_ref[head], preferred_element_type=jnp.float32)
            term = jnp.maximum(product, 0.0) * weight[head : head + 1, :]
            total = term if total is None else total + term
        out_ref[pl.ds(first, count)] = total


def index_partial(index_key, index_query, index_weight):
    tokens = index_key.shape[0]
    rows, heads, width = index_query.shape
    tile = min(tokens, 1024)
    return pl.pallas_call(
        index_kernel,
        grid=(tokens // tile,),
        in_specs=[
            pl.BlockSpec((tile, width), lambda i: (i, 0)),
            pl.BlockSpec((rows, heads, width), lambda i: (0, 0, 0)),
            pl.BlockSpec((heads, rows), lambda i: (0, 0)),
        ],
        out_specs=pl.BlockSpec((tile, rows), lambda i: (i, 0)),
        scratch_shapes=[
            pltpu.VMEM((rows, heads, width), jnp.float32),
            pltpu.VMEM((heads, width, rows), jnp.bfloat16),
        ],
        out_shape=jax.ShapeDtypeStruct((tokens, rows), jnp.float32),
        compiler_params=pltpu.CompilerParams(vmem_limit_bytes=VMEM_LIMIT),
        cost_estimate=pl.CostEstimate(
            flops=4 * tokens * rows * heads * width,
            bytes_accessed=4 * tokens * rows,
            transcendentals=0,
        ),
        name="indexer",
    )(index_key, index_query, jnp.transpose(index_weight))


def attend_kernel(
    chunk,
    groups,
    offset_ref,
    count_ref,
    slot_ref,
    query_hbm,
    cosine_ref,
    sine_ref,
    own_hbm,
    peer_hbm,
    out_ref,
    level_ref,
    stage_ref,
    turned_ref,
    value_ref,
    raw_ref,
    query_ref,
    part_ref,
    stat_ref,
    item_ref,
    start_ref,
    sems,
):
    rows, heads, width = query_ref.shape
    tokens = own_hbm.shape[1]
    half = DR // 2
    piece = stage_ref.shape[2]
    pieces = 2 * tokens // piece
    offset = offset_ref[0]
    tile = pl.multiple_of(offset // 128 * 128, 128)
    inside = offset - tile

    def cache_copy(number):
        source = own_hbm if number * piece < tokens else peer_hbm
        return pltpu.make_async_copy(
            source.at[:, pl.ds(number * piece % tokens, piece)],
            stage_ref.at[number % 2],
            sems.at[number % 2],
        )

    query_copy = pltpu.make_async_copy(query_hbm.at[:, :, pl.ds(tile, 128)], raw_ref, sems.at[2])
    cache_copy(0).start()
    query_copy.start()
    cache_copy(1).start()

    def list_row(row, filled):
        start_ref[row] = filled
        for part in range(groups):
            item_ref[filled + part] = row * groups + part
        return filled + count_ref[0, offset + row]

    start_ref[rows] = lax.fori_loop(0, rows, list_row, 0)

    deep = width
    low_half = lax.broadcasted_iota(jnp.int32, (deep, 2 * BS), 1) < BS

    for number in range(pieces):
        cache_copy(number).wait()

        def turn(index, carry, number=number):
            both = stage_ref[number % 2, :, pl.ds(pl.multiple_of(index * 128, 128), 128)]
            swapped = jnp.concatenate([both[:, BS:], both[:, :BS]], axis=1)
            block = number * (piece // BS) + 2 * index
            turned_ref[block] = jnp.where(low_half, both, swapped)
            turned_ref[block + 1] = jnp.where(low_half, swapped, both)
            values = both[:LATENT_WIDTH].T
            value_ref[block] = values[:BS]
            value_ref[block + 1] = values[BS:]
            return carry

        lax.fori_loop(0, piece // 128, turn, 0)
        if number + 2 < pieces:
            cache_copy(number + 2).start()

    query_copy.wait()
    cosine = cosine_ref[:, pl.ds(tile, 128)]
    sine = sine_ref[:, pl.ds(tile, 128)]

    def turn_query(block, carry):
        for head in range(8):
            raw = raw_ref[block * 8 + head].astype(jnp.float32)
            first = raw[LATENT_WIDTH : LATENT_WIDTH + half]
            second = raw[LATENT_WIDTH + half :]
            rotated = jnp.concatenate(
                [
                    raw[:LATENT_WIDTH],
                    first * cosine - second * sine,
                    second * cosine + first * sine,
                ],
                axis=0,
            ).astype(jnp.bfloat16).T.astype(jnp.float32)
            picked = rotated[:rows]
            for place in range(1, 128 // rows):
                picked = jnp.where(
                    inside == place * rows, rotated[place * rows : (place + 1) * rows], picked
                )
            query_ref[:, block * 8 + head, :] = picked
        return carry

    lax.fori_loop(0, heads // 8, turn_query, 0)

    out_lane = lax.broadcasted_iota(jnp.int32, (heads, 128), 1)
    wide = LATENT_WIDTH // 128
    batch = part_ref.shape[0] // groups

    def attend_batch(number, stats):
        base = start_ref[number * batch]
        stop = start_ref[(number + 1) * batch]

        def names_of(item):
            code = item_ref[item]
            row = code // groups
            part = code % groups
            return row, [slot_ref[part * chunk + j, offset + row] for j in range(chunk)]

        def scores_of(item):
            row, names = names_of(item)
            keys = jnp.concatenate(
                [
                    jnp.where(low_half, turned_ref[names[j]], turned_ref[names[j + 1]])
                    for j in range(0, chunk, 2)
                ],
                axis=1,
            )
            return jnp.dot(
                query_ref[row].astype(jnp.bfloat16), keys, preferred_element_type=jnp.float32
            )

        def softmax_of(scores):
            top = jnp.max(scores, axis=1, keepdims=True)
            weights = jnp.exp2((scores - top) * EXP_SCALE)
            return top, jnp.sum(weights, axis=1, keepdims=True), weights.astype(jnp.bfloat16)

        def numer_of(item, weights):
            _, names = names_of(item)
            values = jnp.concatenate([value_ref[name] for name in names], axis=0)
            return jnp.dot(weights, values, preferred_element_type=jnp.float32)

        def keep(item, top, total, numer):
            part_ref[item - base] = numer
            stat_ref[0, item - base] = jnp.broadcast_to(top, (heads, 128))
            stat_ref[1, item - base] = jnp.broadcast_to(total, (heads, 128))

        def item_at(index, unrolled):
            return jnp.minimum(base + index * UNROLL + unrolled, stop - 1)

        def step(index, carry):
            items = [item_at(index, u) for u in range(UNROLL)]
            scores = [scores_of(item) for item in items]
            soft = [softmax_of(s) for s in scores]
            numers = [numer_of(item, s[2]) for item, s in zip(items, soft)]
            for item, (top, total, _), numer in zip(items, soft, numers):
                keep(item, top, total, numer)
            return carry

        lax.fori_loop(0, (stop - base + UNROLL - 1) // UNROLL, step, 0)

        def merge_row(row):
            count = count_ref[0, offset + row]
            first = start_ref[row] - base
            places = [
                jnp.maximum(first + jnp.minimum(part, count - 1), 0) for part in range(groups)
            ]
            peaks = [
                jnp.where(part < count, stat_ref[0, places[part]], NEG) for part in range(groups)
            ]
            peak = functools.reduce(jnp.maximum, peaks)
            factors = [
                jnp.where(part < count, jnp.exp2((peaks[part] - peak) * EXP_SCALE), 0.0)
                for part in range(groups)
            ]
            total = sum(
                jnp.where(part < count, factors[part] * stat_ref[1, places[part]], 0.0)
                for part in range(groups)
            )
            inverse = jnp.where(count > 0, 1.0 / total, 0.0)
            merged = sum(
                jnp.where(
                    part < count,
                    part_ref[places[part]]
                    * jnp.concatenate([factors[part] * inverse] * wide, axis=1),
                    0.0,
                )
                for part in range(groups)
            )
            return merged.astype(jnp.bfloat16), peak, total

        def merge_rows(index, carry):
            tops, totals = carry
            found = [number * batch + index * MERGE + u for u in range(MERGE)]
            merged = [merge_row(row) for row in found]
            for row, (out, peak, total) in zip(found, merged):
                out_ref[row] = out
                here = out_lane == row
                tops = jnp.where(here, peak, tops)
                totals = jnp.where(here, total, totals)
            return tops, totals

        return lax.fori_loop(0, batch // MERGE, merge_rows, stats)

    blank = jnp.zeros((heads, 128), jnp.float32)
    tops, totals = lax.fori_loop(0, rows // batch, attend_batch, (blank, blank))
    level_ref[0] = tops
    level_ref[1] = totals


def attend(offset, counts, slots, query, cosine, sine, own, peer, rows, chunk, groups):
    heads, width = query.shape[0], query.shape[1]
    tokens = own.shape[1]
    blocks = tokens // BS
    smem = pl.BlockSpec(memory_space=pltpu.SMEM)
    vmem = pl.BlockSpec(memory_space=pltpu.VMEM)
    hbm = pl.BlockSpec(memory_space=pl.ANY)
    batch = min(rows, 32)
    return pl.pallas_call(
        functools.partial(attend_kernel, chunk, groups),
        out_shape=(
            jax.ShapeDtypeStruct((rows, heads, LATENT_WIDTH), jnp.bfloat16),
            jax.ShapeDtypeStruct((2, heads, 128), jnp.float32),
        ),
        in_specs=[smem, smem, smem, hbm, vmem, vmem, hbm, hbm],
        out_specs=(vmem, vmem),
        scratch_shapes=[
            pltpu.VMEM((2, width, tokens // 2), jnp.bfloat16),
            pltpu.VMEM((2 * blocks, width, 2 * BS), jnp.bfloat16),
            pltpu.VMEM((2 * blocks, BS, LATENT_WIDTH), jnp.bfloat16),
            pltpu.VMEM((heads, width, 128), jnp.bfloat16),
            pltpu.VMEM((rows, heads, width), jnp.float32),
            pltpu.VMEM((batch * groups, heads, LATENT_WIDTH), jnp.float32),
            pltpu.VMEM((2, batch * groups, heads, 128), jnp.float32),
            pltpu.SMEM((rows * groups + groups,), jnp.int32),
            pltpu.SMEM((rows + 1,), jnp.int32),
            pltpu.SemaphoreType.DMA((3,)),
        ],
        compiler_params=pltpu.CompilerParams(vmem_limit_bytes=VMEM_LIMIT),
        cost_estimate=pl.CostEstimate(
            flops=40 * 10**9, bytes_accessed=16 * 2**20, transcendentals=2 * 10**6
        ),
        name="attend",
    )(offset, counts, slots, query, cosine, sine, own, peer)


def chip_slots(block_ids, own_segment, peer_segment, blocks, chunk, groups):
    ids = jnp.transpose(block_ids)
    segment = ids // blocks
    local = ids % blocks
    place_of = jnp.where(segment == peer_segment, local + blocks, local)
    owned = (segment == own_segment) | (segment == peer_segment)
    count = ids.shape[0]
    before = jnp.tril(jnp.ones((count, count), jnp.float32), -1)
    place = jnp.dot(before, owned.astype(jnp.float32)).astype(jnp.int32)
    place = jnp.where(owned, place, -1)
    wanted = jnp.arange(groups * chunk, dtype=jnp.int32)
    slots = jnp.sum(
        jnp.where(place[:, None, :] == wanted[None, :, None], place_of[:, None, :], 0), axis=0
    )
    counts = jnp.sum(owned.astype(jnp.int32), axis=0, keepdims=True) // chunk
    return counts, slots


def per_device(
    cache_latent, index_key, query_latent, index_query, index_weight, block_ids, stretch_start
):
    shards = lax.axis_size("ctx")
    me = lax.axis_index("ctx")
    pairs = shards // 2
    core = me % 2
    pair = me // 2
    total_rows = query_latent.shape[0]
    rows = total_rows // shards
    chunk = block_ids.shape[1] // shards
    groups = 2 + min(2, shards // 4)
    blocks = cache_latent.shape[0] // BS

    own = jnp.transpose(cache_latent)
    peer = lax.ppermute(own, "ctx", [(i, i ^ 1) for i in range(shards)])
    partial = index_partial(index_key, index_query, index_weight)
    index_scores = lax.psum_scatter(partial, "head", scatter_dimension=0, tiled=True)
    query = jnp.transpose(query_latent, (1, 2, 0))
    cosine, sine = rope_tables(total_rows, stretch_start)
    counts, slots = chip_slots(block_ids, me, me ^ 1, blocks, chunk, groups)

    def attend_for(owner):
        offset = (owner * rows).astype(jnp.int32).reshape(1)
        return attend(
            offset, counts, slots, query, cosine, sine, own, peer, rows, chunk, groups
        )

    parts = []
    for ahead in range(1, pairs):
        owner = ((pair + ahead) % pairs) * 2 + core
        moves = [(i, ((i // 2 + ahead) % pairs) * 2 + i % 2) for i in range(shards)]
        parts.append([lax.ppermute(part, "ctx", moves) for part in attend_for(owner)])
    parts.append(attend_for(me))

    peak = functools.reduce(jnp.maximum, [part[1][0] for part in parts])
    shares = [jnp.exp2((part[1][0] - peak) * EXP_SCALE) * part[1][1] for part in parts]
    whole = sum(shares)
    attended = sum(
        part[0].astype(jnp.float32) * jnp.transpose((share / whole)[:, :rows])[:, :, None]
        for part, share in zip(parts, shares)
    )
    return (index_scores, attended.astype(jnp.bfloat16))


def solution(mesh):
    in_specs = (
        P(("groups", "ctx"), None),
        P(("groups", "ctx"), None),
        P("groups", "head", None),
        P("groups", "head", None),
        P("groups", "head"),
        P("groups", None),
        P("groups"),
    )
    out_specs = (P(("groups", "ctx", "head"), None), P(("groups", "ctx"), "head", None))
    return jax.shard_map(
        per_device, mesh=mesh, in_specs=in_specs, out_specs=out_specs, check_vma=False
    )
```

```python
import functools

import jax
import jax.numpy as jnp
from jax import lax
from jax.experimental import pallas as pl
from jax.experimental.pallas import tpu as pltpu
from jax.sharding import PartitionSpec as P

LATENT_WIDTH = 512
DR = 64
ID = 128
QKD = 192
BS = 64
NEG = -1e30
EXP_SCALE = QKD**-0.5 * 1.4426950408889634
UNROLL = 8
MERGE = 4
TURN = 4
VMEM_LIMIT = 58 * 2**20


def rope_tables(rows, stretch_start):
    half = DR // 2
    positions = (stretch_start[0] + jnp.arange(rows, dtype=jnp.int32)).astype(jnp.float32)
    freqs = 10000.0 ** (-jnp.arange(half, dtype=jnp.float32) / half)
    angle = positions[None, :] * freqs[:, None]
    return jnp.cos(angle), jnp.sin(angle)


def index_kernel(key_ref, query_ref, weight_ref, out_ref, wide_ref, turned_ref):
    heads = turned_ref.shape[0]
    tile = key_ref.shape[0]

    @pl.when(pl.program_id(0) == 0)
    def _():
        wide_ref[...] = query_ref[...].astype(jnp.float32)
        for head in range(heads):
            turned_ref[head] = wide_ref[:, head, :].T.astype(jnp.bfloat16)

    weight = weight_ref[...].astype(jnp.float32) * ID ** (-0.5)
    count = min(tile, 128)
    for first in range(0, tile, count):
        keys = key_ref[pl.ds(first, count)]
        total = None
        for head in range(heads):
            product = jnp.dot(keys, turned_ref[head], preferred_element_type=jnp.float32)
            term = jnp.maximum(product, 0.0) * weight[head : head + 1, :]
            total = term if total is None else total + term
        out_ref[pl.ds(first, count)] = total


def index_partial(index_key, index_query, index_weight):
    tokens = index_key.shape[0]
    rows, heads, width = index_query.shape
    tile = min(tokens, 1024)
    return pl.pallas_call(
        index_kernel,
        grid=(tokens // tile,),
        in_specs=[
            pl.BlockSpec((tile, width), lambda i: (i, 0)),
            pl.BlockSpec((rows, heads, width), lambda i: (0, 0, 0)),
            pl.BlockSpec((heads, rows), lambda i: (0, 0)),
        ],
        out_specs=pl.BlockSpec((tile, rows), lambda i: (i, 0)),
        scratch_shapes=[
            pltpu.VMEM((rows, heads, width), jnp.float32),
            pltpu.VMEM((heads, width, rows), jnp.bfloat16),
        ],
        out_shape=jax.ShapeDtypeStruct((tokens, rows), jnp.float32),
        compiler_params=pltpu.CompilerParams(vmem_limit_bytes=VMEM_LIMIT),
        cost_estimate=pl.CostEstimate(
            flops=4 * tokens * rows * heads * width,
            bytes_accessed=4 * tokens * rows,
            transcendentals=0,
        ),
        name="indexer",
    )(index_key, index_query, jnp.transpose(index_weight))


def attend_kernel(
    chunk,
    groups,
    offset_ref,
    count_ref,
    slot_ref,
    query_hbm,
    cosine_ref,
    sine_ref,
    own_hbm,
    peer_hbm,
    out_ref,
    level_ref,
    stage_ref,
    turned_ref,
    value_ref,
    raw_ref,
    query_ref,
    part_ref,
    stat_ref,
    item_ref,
    start_ref,
    sems,
):
    rows, heads, width = query_ref.shape
    tokens = own_hbm.shape[1]
    half = DR // 2
    piece = stage_ref.shape[2]
    pieces = 2 * tokens // piece
    offset = offset_ref[0]
    tile = pl.multiple_of(offset // 128 * 128, 128)
    inside = offset - tile

    def cache_copy(number):
        source = own_hbm if number * piece < tokens else peer_hbm
        return pltpu.make_async_copy(
            source.at[:, pl.ds(number * piece % tokens, piece)],
            stage_ref.at[number],
            sems.at[number],
        )

    query_copy = pltpu.make_async_copy(query_hbm.at[:, :, pl.ds(tile, 128)], raw_ref, sems.at[4])
    cache_copy(0).start()
    for number in range(1, pieces):
        cache_copy(number).start()
    query_copy.start()

    def list_row(row, filled):
        start_ref[row] = filled
        for part in range(groups):
            item_ref[filled + part] = row * groups + part
        return filled + count_ref[0, offset + row]

    start_ref[rows] = lax.fori_loop(0, rows, list_row, 0)

    deep = width
    low_half = lax.broadcasted_iota(jnp.int32, (deep, 2 * BS), 1) < BS

    for number in range(pieces):
        cache_copy(number).wait()

        def turn_one(index, number=number):
            both = stage_ref[number, :, pl.ds(pl.multiple_of(index * 128, 128), 128)]
            swapped = jnp.concatenate([both[:, BS:], both[:, :BS]], axis=1)
            block = number * (piece // BS) + 2 * index
            turned_ref[block] = jnp.where(low_half, both, swapped)
            turned_ref[block + 1] = jnp.where(low_half, swapped, both)
            values = both[:LATENT_WIDTH].T
            value_ref[block] = values[:BS]
            value_ref[block + 1] = values[BS:]

        def turn(index, carry, number=number):
            for unrolled in range(TURN):
                turn_one(index * TURN + unrolled, number)
            return carry

        lax.fori_loop(0, piece // 128 // TURN, turn, 0)

    query_copy.wait()
    cosine = cosine_ref[:, pl.ds(tile, 128)]
    sine = sine_ref[:, pl.ds(tile, 128)]

    def turn_query(block, carry):
        for head in range(8):
            raw = raw_ref[block * 8 + head].astype(jnp.float32)
            first = raw[LATENT_WIDTH : LATENT_WIDTH + half]
            second = raw[LATENT_WIDTH + half :]
            rotated = jnp.concatenate(
                [
                    raw[:LATENT_WIDTH],
                    first * cosine - second * sine,
                    second * cosine + first * sine,
                ],
                axis=0,
            ).astype(jnp.bfloat16).T.astype(jnp.float32)
            picked = rotated[:rows]
            for place in range(1, 128 // rows):
                picked = jnp.where(
                    inside == place * rows, rotated[place * rows : (place + 1) * rows], picked
                )
            query_ref[:, block * 8 + head, :] = picked
        return carry

    lax.fori_loop(0, heads // 8, turn_query, 0)

    out_lane = lax.broadcasted_iota(jnp.int32, (heads, 128), 1)
    wide = LATENT_WIDTH // 128
    batch = part_ref.shape[0] // groups

    def attend_batch(number, stats):
        base = start_ref[number * batch]
        stop = start_ref[(number + 1) * batch]

        def names_of(item):
            code = item_ref[item]
            row = code // groups
            part = code % groups
            return row, [slot_ref[part * chunk + j, offset + row] for j in range(chunk)]

        def scores_of(item):
            row, names = names_of(item)
            keys = jnp.concatenate(
                [
                    jnp.where(low_half, turned_ref[names[j]], turned_ref[names[j + 1]])
                    for j in range(0, chunk, 2)
                ],
                axis=1,
            )
            return jnp.dot(
                query_ref[row].astype(jnp.bfloat16), keys, preferred_element_type=jnp.float32
            )

        def softmax_of(scores):
            top = jnp.max(scores, axis=1, keepdims=True)
            weights = jnp.exp2((scores - top) * EXP_SCALE)
            return top, jnp.sum(weights, axis=1, keepdims=True), weights.astype(jnp.bfloat16)

        def numer_of(item, weights):
            _, names = names_of(item)
            values = jnp.concatenate([value_ref[name] for name in names], axis=0)
            return jnp.dot(weights, values, preferred_element_type=jnp.float32)

        def keep(item, top, total, numer):
            part_ref[item - base] = numer
            stat_ref[0, item - base] = jnp.broadcast_to(top, (heads, 128))
            stat_ref[1, item - base] = jnp.broadcast_to(total, (heads, 128))

        def item_at(index, unrolled):
            return jnp.minimum(base + index * UNROLL + unrolled, stop - 1)

        def step(index, carry):
            items = [item_at(index, u) for u in range(UNROLL)]
            scores = [scores_of(item) for item in items]
            soft = [softmax_of(s) for s in scores]
            numers = [numer_of(item, s[2]) for item, s in zip(items, soft)]
            for item, (top, total, _), numer in zip(items, soft, numers):
                keep(item, top, total, numer)
            return carry

        lax.fori_loop(0, (stop - base + UNROLL - 1) // UNROLL, step, 0)

        def merge_row(row):
            count = count_ref[0, offset + row]
            first = start_ref[row] - base
            places = [
                jnp.maximum(first + jnp.minimum(part, count - 1), 0) for part in range(groups)
            ]
            peaks = [
                jnp.where(part < count, stat_ref[0, places[part]], NEG) for part in range(groups)
            ]
            peak = functools.reduce(jnp.maximum, peaks)
            factors = [
                jnp.where(part < count, jnp.exp2((peaks[part] - peak) * EXP_SCALE), 0.0)
                for part in range(groups)
            ]
            total = sum(factors[part] * stat_ref[1, places[part]] for part in range(groups))
            total = jnp.where(count > 0, total, 0.0)
            inverse = jnp.where(count > 0, 1.0 / total, 0.0)
            merged = sum(
                part_ref[places[part]] * jnp.concatenate([factors[part] * inverse] * wide, axis=1)
                for part in range(groups)
            )
            merged = jnp.where(count > 0, merged, 0.0)
            return merged.astype(jnp.bfloat16), peak, total

        def merge_rows(index, carry):
            tops, totals = carry
            found = [number * batch + index * MERGE + u for u in range(MERGE)]
            merged = [merge_row(row) for row in found]
            for row, (out, peak, total) in zip(found, merged):
                out_ref[row] = out
                here = out_lane == row
                tops = jnp.where(here, peak, tops)
                totals = jnp.where(here, total, totals)
            return tops, totals

        return lax.fori_loop(0, batch // MERGE, merge_rows, stats)

    blank = jnp.zeros((heads, 128), jnp.float32)
    tops, totals = lax.fori_loop(0, rows // batch, attend_batch, (blank, blank))
    level_ref[0] = tops
    level_ref[1] = totals


def attend(offset, counts, slots, query, cosine, sine, own, peer, rows, chunk, groups):
    heads, width = query.shape[0], query.shape[1]
    tokens = own.shape[1]
    blocks = tokens // BS
    smem = pl.BlockSpec(memory_space=pltpu.SMEM)
    vmem = pl.BlockSpec(memory_space=pltpu.VMEM)
    hbm = pl.BlockSpec(memory_space=pl.ANY)
    batch = min(rows, 32)
    return pl.pallas_call(
        functools.partial(attend_kernel, chunk, groups),
        out_shape=(
            jax.ShapeDtypeStruct((rows, heads, LATENT_WIDTH), jnp.bfloat16),
            jax.ShapeDtypeStruct((2, heads, 128), jnp.float32),
        ),
        in_specs=[smem, smem, smem, hbm, vmem, vmem, hbm, hbm],
        out_specs=(vmem, vmem),
        scratch_shapes=[
            pltpu.VMEM((4, width, tokens // 2), jnp.bfloat16),
            pltpu.VMEM((2 * blocks, width, 2 * BS), jnp.bfloat16),
            pltpu.VMEM((2 * blocks, BS, LATENT_WIDTH), jnp.bfloat16),
            pltpu.VMEM((heads, width, 128), jnp.bfloat16),
            pltpu.VMEM((rows, heads, width), jnp.float32),
            pltpu.VMEM((batch * groups, heads, LATENT_WIDTH), jnp.float32),
            pltpu.VMEM((2, batch * groups, heads, 128), jnp.float32),
            pltpu.SMEM((rows * groups + groups,), jnp.int32),
            pltpu.SMEM((rows + 1,), jnp.int32),
            pltpu.SemaphoreType.DMA((5,)),
        ],
        compiler_params=pltpu.CompilerParams(vmem_limit_bytes=VMEM_LIMIT),
        cost_estimate=pl.CostEstimate(
            flops=40 * 10**9, bytes_accessed=16 * 2**20, transcendentals=2 * 10**6
        ),
        name="attend",
    )(offset, counts, slots, query, cosine, sine, own, peer)


def chip_slots(block_ids, own_segment, peer_segment, blocks, chunk, groups):
    ids = jnp.transpose(block_ids)
    segment = ids // blocks
    local = ids % blocks
    place_of = jnp.where(segment == peer_segment, local + blocks, local)
    owned = (segment == own_segment) | (segment == peer_segment)
    count = ids.shape[0]
    before = jnp.tril(jnp.ones((count, count), jnp.float32), -1)
    place = jnp.dot(before, owned.astype(jnp.float32)).astype(jnp.int32)
    place = jnp.where(owned, place, -1)
    wanted = jnp.arange(groups * chunk, dtype=jnp.int32)
    slots = jnp.sum(
        jnp.where(place[:, None, :] == wanted[None, :, None], place_of[:, None, :], 0), axis=0
    )
    counts = jnp.sum(owned.astype(jnp.int32), axis=0, keepdims=True) // chunk
    return counts, slots


def per_device(
    cache_latent, index_key, query_latent, index_query, index_weight, block_ids, stretch_start
):
    shards = lax.axis_size("ctx")
    me = lax.axis_index("ctx")
    pairs = shards // 2
    core = me % 2
    pair = me // 2
    total_rows = query_latent.shape[0]
    rows = total_rows // shards
    chunk = block_ids.shape[1] // shards
    groups = 2 + min(2, shards // 4)
    blocks = cache_latent.shape[0] // BS

    own = jnp.transpose(cache_latent)
    peer = lax.ppermute(own, "ctx", [(i, i ^ 1) for i in range(shards)])
    partial = index_partial(index_key, index_query, index_weight)
    index_scores = lax.psum_scatter(partial, "head", scatter_dimension=0, tiled=True)
    query = jnp.transpose(query_latent, (1, 2, 0))
    cosine, sine = rope_tables(total_rows, stretch_start)
    counts, slots = chip_slots(block_ids, me, me ^ 1, blocks, chunk, groups)

    def attend_for(owner):
        offset = (owner * rows).astype(jnp.int32).reshape(1)
        return attend(
            offset, counts, slots, query, cosine, sine, own, peer, rows, chunk, groups
        )

    parts = []
    for ahead in range(1, pairs):
        owner = ((pair + ahead) % pairs) * 2 + core
        moves = [(i, ((i // 2 + ahead) % pairs) * 2 + i % 2) for i in range(shards)]
        parts.append([lax.ppermute(part, "ctx", moves) for part in attend_for(owner)])
    parts.append(attend_for(me))

    peak = functools.reduce(jnp.maximum, [part[1][0] for part in parts])
    shares = [jnp.exp2((part[1][0] - peak) * EXP_SCALE) * part[1][1] for part in parts]
    whole = sum(shares)
    attended = sum(
        part[0].astype(jnp.float32) * jnp.transpose((share / whole)[:, :rows])[:, :, None]
        for part, share in zip(parts, shares)
    )
    return (index_scores, attended.astype(jnp.bfloat16))


def solution(mesh):
    in_specs = (
        P(("groups", "ctx"), None),
        P(("groups", "ctx"), None),
        P("groups", "head", None),
        P("groups", "head", None),
        P("groups", "head"),
        P("groups", None),
        P("groups"),
    )
    out_specs = (P(("groups", "ctx", "head"), None), P(("groups", "ctx"), "head", None))
    return jax.shard_map(
        per_device, mesh=mesh, in_specs=in_specs, out_specs=out_specs, check_vma=False
    )
```

```python
import functools

import jax
import jax.numpy as jnp
from jax import lax
from jax.experimental import pallas as pl
from jax.experimental.pallas import tpu as pltpu
from jax.sharding import PartitionSpec as P

LATENT_WIDTH = 512
DR = 64
ID = 128
QKD = 192
BS = 64
NEG = -1e30
EXP_SCALE = QKD**-0.5 * 1.4426950408889634
UNROLL = 8
MERGE = 4
TAIL = 3
TURN = 4
VMEM_LIMIT = 58 * 2**20


def rope_tables(rows, stretch_start):
    half = DR // 2
    positions = (stretch_start[0] + jnp.arange(rows, dtype=jnp.int32)).astype(jnp.float32)
    freqs = 10000.0 ** (-jnp.arange(half, dtype=jnp.float32) / half)
    angle = positions[None, :] * freqs[:, None]
    return jnp.cos(angle), jnp.sin(angle)


def index_kernel(key_ref, query_ref, weight_ref, out_ref, wide_ref, turned_ref):
    heads = turned_ref.shape[0]
    tile = key_ref.shape[0]

    @pl.when(pl.program_id(0) == 0)
    def _():
        wide_ref[...] = query_ref[...].astype(jnp.float32)
        for head in range(heads):
            turned_ref[head] = wide_ref[:, head, :].T.astype(jnp.bfloat16)

    weight = weight_ref[...].astype(jnp.float32) * ID ** (-0.5)
    count = min(tile, 128)
    for first in range(0, tile, count):
        keys = key_ref[pl.ds(first, count)]
        total = None
        for head in range(heads):
            product = jnp.dot(keys, turned_ref[head], preferred_element_type=jnp.float32)
            term = jnp.maximum(product, 0.0) * weight[head : head + 1, :]
            total = term if total is None else total + term
        out_ref[pl.ds(first, count)] = total


def index_partial(index_key, index_query, index_weight):
    tokens = index_key.shape[0]
    rows, heads, width = index_query.shape
    tile = min(tokens, 1024)
    return pl.pallas_call(
        index_kernel,
        grid=(tokens // tile,),
        in_specs=[
            pl.BlockSpec((tile, width), lambda i: (i, 0)),
            pl.BlockSpec((rows, heads, width), lambda i: (0, 0, 0)),
            pl.BlockSpec((heads, rows), lambda i: (0, 0)),
        ],
        out_specs=pl.BlockSpec((tile, rows), lambda i: (i, 0)),
        scratch_shapes=[
            pltpu.VMEM((rows, heads, width), jnp.float32),
            pltpu.VMEM((heads, width, rows), jnp.bfloat16),
        ],
        out_shape=jax.ShapeDtypeStruct((tokens, rows), jnp.float32),
        compiler_params=pltpu.CompilerParams(vmem_limit_bytes=VMEM_LIMIT),
        cost_estimate=pl.CostEstimate(
            flops=4 * tokens * rows * heads * width,
            bytes_accessed=4 * tokens * rows,
            transcendentals=0,
        ),
        name="indexer",
    )(index_key, index_query, jnp.transpose(index_weight))


def attend_kernel(
    chunk,
    groups,
    offset_ref,
    count_ref,
    slot_ref,
    query_hbm,
    cosine_ref,
    sine_ref,
    own_hbm,
    peer_hbm,
    out_ref,
    level_ref,
    stage_ref,
    turned_ref,
    value_ref,
    raw_ref,
    query_ref,
    part_ref,
    stat_ref,
    item_ref,
    start_ref,
    sems,
):
    rows, heads, width = query_ref.shape
    tokens = own_hbm.shape[1]
    half = DR // 2
    piece = stage_ref.shape[2]
    pieces = 2 * tokens // piece
    offset = offset_ref[0]
    tile = pl.multiple_of(offset // 128 * 128, 128)
    inside = offset - tile

    def cache_copy(number):
        source = own_hbm if number * piece < tokens else peer_hbm
        return pltpu.make_async_copy(
            source.at[:, pl.ds(number * piece % tokens, piece)],
            stage_ref.at[number],
            sems.at[number],
        )

    query_copy = pltpu.make_async_copy(query_hbm.at[:, :, pl.ds(tile, 128)], raw_ref, sems.at[4])
    cache_copy(0).start()
    for number in range(1, pieces):
        cache_copy(number).start()
    query_copy.start()

    def list_row(row, filled):
        start_ref[row] = filled
        for part in range(groups):
            item_ref[filled + part] = row * groups + part
        return filled + count_ref[0, offset + row]

    start_ref[rows] = lax.fori_loop(0, rows, list_row, 0)

    deep = width
    low_half = lax.broadcasted_iota(jnp.int32, (deep, 2 * BS), 1) < BS

    for number in range(pieces):
        cache_copy(number).wait()

        def turn_one(index, number=number):
            both = stage_ref[number, :, pl.ds(pl.multiple_of(index * 128, 128), 128)]
            swapped = jnp.concatenate([both[:, BS:], both[:, :BS]], axis=1)
            block = number * (piece // BS) + 2 * index
            turned_ref[block] = jnp.where(low_half, both, swapped)
            turned_ref[block + 1] = jnp.where(low_half, swapped, both)
            values = both[:LATENT_WIDTH].T
            value_ref[block] = values[:BS]
            value_ref[block + 1] = values[BS:]

        def turn(index, carry, number=number):
            for unrolled in range(TURN):
                turn_one(index * TURN + unrolled, number)
            return carry

        lax.fori_loop(0, piece // 128 // TURN, turn, 0)

    query_copy.wait()
    cosine = cosine_ref[:, pl.ds(tile, 128)]
    sine = sine_ref[:, pl.ds(tile, 128)]

    def turn_query(block, carry):
        for head in range(8):
            raw = raw_ref[block * 8 + head].astype(jnp.float32)
            first = raw[LATENT_WIDTH : LATENT_WIDTH + half]
            second = raw[LATENT_WIDTH + half :]
            rotated = jnp.concatenate(
                [
                    raw[:LATENT_WIDTH],
                    first * cosine - second * sine,
                    second * cosine + first * sine,
                ],
                axis=0,
            ).astype(jnp.bfloat16).T.astype(jnp.float32)
            picked = rotated[:rows]
            for place in range(1, 128 // rows):
                picked = jnp.where(
                    inside == place * rows, rotated[place * rows : (place + 1) * rows], picked
                )
            query_ref[:, block * 8 + head, :] = picked
        return carry

    lax.fori_loop(0, heads // 8, turn_query, 0)

    out_lane = lax.broadcasted_iota(jnp.int32, (heads, 128), 1)
    wide = LATENT_WIDTH // 128
    batch = part_ref.shape[0] // groups

    def attend_batch(number, stats):
        base = start_ref[number * batch]
        stop = start_ref[(number + 1) * batch]

        def names_of(item):
            code = item_ref[item]
            row = code // groups
            part = code % groups
            return row, [slot_ref[part * chunk + j, offset + row] for j in range(chunk)]

        def scores_of(item):
            row, names = names_of(item)
            keys = jnp.concatenate(
                [
                    jnp.where(low_half, turned_ref[names[j]], turned_ref[names[j + 1]])
                    for j in range(0, chunk, 2)
                ],
                axis=1,
            )
            return jnp.dot(
                query_ref[row].astype(jnp.bfloat16), keys, preferred_element_type=jnp.float32
            )

        def softmax_of(scores):
            top = jnp.max(scores, axis=1, keepdims=True)
            weights = jnp.exp2((scores - top) * EXP_SCALE)
            return top, jnp.sum(weights, axis=1, keepdims=True), weights.astype(jnp.bfloat16)

        def numer_of(item, weights):
            _, names = names_of(item)
            values = jnp.concatenate([value_ref[name] for name in names], axis=0)
            return jnp.dot(weights, values, preferred_element_type=jnp.float32)

        def keep(item, top, total, numer):
            part_ref[item - base] = numer
            stat_ref[0, item - base] = jnp.broadcast_to(top, (heads, 128))
            stat_ref[1, item - base] = jnp.broadcast_to(total, (heads, 128))

        def steps(first, count, unroll):
            def step(index, carry):
                items = [
                    jnp.minimum(first + index * unroll + u, stop - 1) for u in range(unroll)
                ]
                scores = [scores_of(item) for item in items]
                soft = [softmax_of(s) for s in scores]
                numers = [numer_of(item, s[2]) for item, s in zip(items, soft)]
                for item, (top, total, _), numer in zip(items, soft, numers):
                    keep(item, top, total, numer)
                return carry

            lax.fori_loop(0, count, step, 0)

        whole = (stop - base) // UNROLL
        rest = stop - base - whole * UNROLL
        steps(base, whole, UNROLL)
        steps(base + whole * UNROLL, (rest + TAIL - 1) // TAIL, TAIL)

        def merge_row(row):
            count = count_ref[0, offset + row]
            first = start_ref[row] - base
            places = [
                jnp.maximum(first + jnp.minimum(part, count - 1), 0) for part in range(groups)
            ]
            peaks = [
                jnp.where(part < count, stat_ref[0, places[part]], NEG) for part in range(groups)
            ]
            peak = functools.reduce(jnp.maximum, peaks)
            factors = [
                jnp.where(part < count, jnp.exp2((peaks[part] - peak) * EXP_SCALE), 0.0)
                for part in range(groups)
            ]
            total = sum(factors[part] * stat_ref[1, places[part]] for part in range(groups))
            total = jnp.where(count > 0, total, 0.0)
            inverse = jnp.where(count > 0, 1.0 / total, 0.0)
            merged = sum(
                part_ref[places[part]] * jnp.concatenate([factors[part] * inverse] * wide, axis=1)
                for part in range(groups)
            )
            merged = jnp.where(count > 0, merged, 0.0)
            return merged.astype(jnp.bfloat16), peak, total

        def merge_rows(index, carry):
            tops, totals = carry
            found = [number * batch + index * MERGE + u for u in range(MERGE)]
            merged = [merge_row(row) for row in found]
            for row, (out, peak, total) in zip(found, merged):
                out_ref[row] = out
                here = out_lane == row
                tops = jnp.where(here, peak, tops)
                totals = jnp.where(here, total, totals)
            return tops, totals

        return lax.fori_loop(0, batch // MERGE, merge_rows, stats)

    blank = jnp.zeros((heads, 128), jnp.float32)
    tops, totals = lax.fori_loop(0, rows // batch, attend_batch, (blank, blank))
    level_ref[0] = tops
    level_ref[1] = totals


def attend(offset, counts, slots, query, cosine, sine, own, peer, rows, chunk, groups):
    heads, width = query.shape[0], query.shape[1]
    tokens = own.shape[1]
    blocks = tokens // BS
    smem = pl.BlockSpec(memory_space=pltpu.SMEM)
    vmem = pl.BlockSpec(memory_space=pltpu.VMEM)
    hbm = pl.BlockSpec(memory_space=pl.ANY)
    batch = min(rows, 32)
    return pl.pallas_call(
        functools.partial(attend_kernel, chunk, groups),
        out_shape=(
            jax.ShapeDtypeStruct((rows, heads, LATENT_WIDTH), jnp.bfloat16),
            jax.ShapeDtypeStruct((2, heads, 128), jnp.float32),
        ),
        in_specs=[smem, smem, smem, hbm, vmem, vmem, hbm, hbm],
        out_specs=(vmem, vmem),
        scratch_shapes=[
            pltpu.VMEM((4, width, tokens // 2), jnp.bfloat16),
            pltpu.VMEM((2 * blocks, width, 2 * BS), jnp.bfloat16),
            pltpu.VMEM((2 * blocks, BS, LATENT_WIDTH), jnp.bfloat16),
            pltpu.VMEM((heads, width, 128), jnp.bfloat16),
            pltpu.VMEM((rows, heads, width), jnp.float32),
            pltpu.VMEM((batch * groups, heads, LATENT_WIDTH), jnp.float32),
            pltpu.VMEM((2, batch * groups, heads, 128), jnp.float32),
            pltpu.SMEM((rows * groups + groups,), jnp.int32),
            pltpu.SMEM((rows + 1,), jnp.int32),
            pltpu.SemaphoreType.DMA((5,)),
        ],
        compiler_params=pltpu.CompilerParams(vmem_limit_bytes=VMEM_LIMIT),
        cost_estimate=pl.CostEstimate(
            flops=40 * 10**9, bytes_accessed=16 * 2**20, transcendentals=2 * 10**6
        ),
        name="attend",
    )(offset, counts, slots, query, cosine, sine, own, peer)


def chip_slots(block_ids, own_segment, peer_segment, blocks, chunk, groups):
    ids = jnp.transpose(block_ids)
    segment = ids // blocks
    local = ids % blocks
    place_of = jnp.where(segment == peer_segment, local + blocks, local)
    owned = (segment == own_segment) | (segment == peer_segment)
    count = ids.shape[0]
    before = jnp.tril(jnp.ones((count, count), jnp.float32), -1)
    place = jnp.dot(before, owned.astype(jnp.float32)).astype(jnp.int32)
    place = jnp.where(owned, place, -1)
    wanted = jnp.arange(groups * chunk, dtype=jnp.int32)
    slots = jnp.sum(
        jnp.where(place[:, None, :] == wanted[None, :, None], place_of[:, None, :], 0), axis=0
    )
    counts = jnp.sum(owned.astype(jnp.int32), axis=0, keepdims=True) // chunk
    return counts, slots


def per_device(
    cache_latent, index_key, query_latent, index_query, index_weight, block_ids, stretch_start
):
    shards = lax.axis_size("ctx")
    me = lax.axis_index("ctx")
    pairs = shards // 2
    core = me % 2
    pair = me // 2
    total_rows = query_latent.shape[0]
    rows = total_rows // shards
    chunk = block_ids.shape[1] // shards
    groups = 2 + min(2, shards // 4)
    blocks = cache_latent.shape[0] // BS

    own = jnp.transpose(cache_latent)
    peer = lax.ppermute(own, "ctx", [(i, i ^ 1) for i in range(shards)])
    partial = index_partial(index_key, index_query, index_weight)
    index_scores = lax.psum_scatter(partial, "head", scatter_dimension=0, tiled=True)
    query = jnp.transpose(query_latent, (1, 2, 0))
    cosine, sine = rope_tables(total_rows, stretch_start)
    counts, slots = chip_slots(block_ids, me, me ^ 1, blocks, chunk, groups)

    def attend_for(owner):
        offset = (owner * rows).astype(jnp.int32).reshape(1)
        return attend(
            offset, counts, slots, query, cosine, sine, own, peer, rows, chunk, groups
        )

    parts = []
    for ahead in range(1, pairs):
        owner = ((pair + ahead) % pairs) * 2 + core
        moves = [(i, ((i // 2 + ahead) % pairs) * 2 + i % 2) for i in range(shards)]
        parts.append([lax.ppermute(part, "ctx", moves) for part in attend_for(owner)])
    parts.append(attend_for(me))

    peak = functools.reduce(jnp.maximum, [part[1][0] for part in parts])
    shares = [jnp.exp2((part[1][0] - peak) * EXP_SCALE) * part[1][1] for part in parts]
    whole = sum(shares)
    attended = sum(
        part[0].astype(jnp.float32) * jnp.transpose((share / whole)[:, :rows])[:, :, None]
        for part, share in zip(parts, shares)
    )
    return (index_scores, attended.astype(jnp.bfloat16))


def solution(mesh):
    in_specs = (
        P(("groups", "ctx"), None),
        P(("groups", "ctx"), None),
        P("groups", "head", None),
        P("groups", "head", None),
        P("groups", "head"),
        P("groups", None),
        P("groups"),
    )
    out_specs = (P(("groups", "ctx", "head"), None), P(("groups", "ctx"), "head", None))
    return jax.shard_map(
        per_device, mesh=mesh, in_specs=in_specs, out_specs=out_specs, check_vma=False
    )
```
